256 devices in a mesh: fsdp: 64 (over z, y, core), tensor: 4 (over x).
Axes of the slice: x: 4, y: 4, z: 8, core: 2. Of those that a mesh axis runs over, the one named last changes fastest.
Arguments:
- gradient: bfloat16 [64, 1024, 1024], P(None, 'fsdp', 'tensor')
- left_stat: float32 [128, 1024, 1024], P('fsdp', 'tensor'), may hold values from -6 to 6
- right_stat: float32 [128, 1024, 1024], P('fsdp', 'tensor'), may hold values from -6 to 6
- left_root: bfloat16 [128, 1024, 1024], P('fsdp', 'tensor')
- right_root: bfloat16 [128, 1024, 1024], P('fsdp', 'tensor')
- block_owner: int32 [64], replicated, may hold values from 0 to 63, as said below
Outputs:
- new_left: float32 [128, 1024, 1024], P('fsdp', 'tensor')
- new_right: float32 [128, 1024, 1024], P('fsdp', 'tensor')
- update: bfloat16 [64, 1024, 1024], P(None, 'fsdp', 'tensor')
The draws below stay inside these ranges and needn't reach their ends.
Inputs may be any that keep to these rules, and one draw needn't show every extreme that they name: `block_owner`: each owner holds at most 2 blocks, and some owner holds exactly 2.
All inputs are finite; a program needn't handle non-finite values.
Results may differ from the reference program's by a relative error of at most 0.0049.
Values may be sent and summed in bfloat16 or wider, within the bound.
No kernel may reach another device: no remote copies, remote signals or barrier semaphores. Data moves between devices by JAX's collectives and lax.ppermute only.
A program may use at most 128 MiB of HBM per device.

```python
import math
import jax
import jax.numpy as jnp
from jax import lax

BS = 1024
SLOTS = 2
NB = 64
N_FSDP = 64


def assemble_factor(offdiag, diagonal):
    rows_index = jnp.arange(BS)[:, None]
    cols_index = jnp.arange(BS)[None, :]
    unit = (rows_index == cols_index).astype(jnp.float32)[None, :, :]
    return offdiag * (1.0 - unit) + diagonal * unit


def draw_gradient(key, part):
    key = jax.random.fold_in(key, 5)
    first, second, third = jax.random.split(key, 3)
    ramp = jnp.arange(BS, dtype=jnp.float32) / BS
    base = jax.random.normal(first, (NB, BS, BS), jnp.float32)
    row_level = jnp.power(10.0, jax.random.uniform(second, (NB, BS, 1), jnp.float32))
    row_scale = row_level * (1.0 + 2.0 * ramp[None, :, None]) / 9.7
    col_scale = jnp.power(10.0, jax.random.uniform(third, (NB, 1, BS), jnp.float32)) / 4.64
    return (0.5 * base * row_scale * col_scale).astype(jnp.bfloat16)


def draw_left_root(key, part):
    key = jax.random.fold_in(key, 11)
    first, second = jax.random.split(key)
    count = NB * SLOTS
    offdiag = 0.02 * jax.random.normal(first, (count, BS, BS), jnp.float32)
    diagonal = jnp.exp(jax.random.uniform(second, (count, BS, 1), jnp.float32, math.log(0.5), math.log(2.0)))
    return assemble_factor(offdiag, diagonal).astype(jnp.bfloat16)


def draw_right_root(key, part):
    key = jax.random.fold_in(key, 17)
    first, second = jax.random.split(key)
    count = NB * SLOTS
    offdiag = 0.02 * jax.random.normal(first, (count, BS, BS), jnp.float32)
    diagonal = jnp.exp(jax.random.uniform(second, (count, BS, 1), jnp.float32, math.log(0.5), math.log(2.0)))
    return assemble_factor(offdiag, diagonal).astype(jnp.bfloat16)


def draw_block_owner(key, part):
    key = jax.random.fold_in(key, 3)
    first, second = jax.random.split(key)
    holders = jax.random.permutation(first, NB)
    doubled = NB // 4
    position = jnp.arange(NB)
    place = jnp.where(position < 2 * doubled, position // 2, position - doubled)
    assigned = holders[place]
    shuffle = jax.random.permutation(second, NB)
    return assigned[shuffle].astype(jnp.int32)


def shard_levels(stream_key, shape, cuts, smallest, largest):
    def one(dim, shards_of):
        steps = jax.random.uniform(jax.random.fold_in(jax.random.fold_in(stream_key, 6), dim), (shards_of,), jnp.float32, smallest / len(cuts), largest / len(cuts))
        return jnp.repeat(jnp.exp(steps), shape[dim] // shards_of).reshape((-1,) + (1,) * (len(shape) - dim - 1))

    level = one(*cuts[0])
    for cut in cuts[1:]:
        level = level * one(*cut)
    return level


def normal_values(key, extent, spread, limit, pieces=(), kind=jnp.bfloat16):
    values = jax.random.normal(key, extent, jnp.float32) * spread
    if len(pieces) > 0:
        values = shard_levels(key, extent, pieces, -0.22, 0.18) * values
    return jnp.clip(values, min=-limit, max=limit).astype(kind)


def setup_inputs(seed: int = 0) -> dict:
    key_of = jax.random.split(jax.random.key(seed), 7)
    return {
        "gradient": draw_gradient(jax.random.fold_in(key_of[6], 71), 0),
        "left_stat": normal_values(key_of[1], (N_FSDP * SLOTS, BS, BS), 1.0, 6.0, ((0, 64), (1, 4)), jnp.float32),
        "right_stat": normal_values(key_of[2], (N_FSDP * SLOTS, BS, BS), 1.0, 6.0, ((0, 64), (1, 4)), jnp.float32),
        "left_root": draw_left_root(jax.random.fold_in(key_of[6], 71), 0),
        "right_root": draw_right_root(jax.random.fold_in(key_of[6], 71), 0),
        "block_owner": draw_block_owner(jax.random.fold_in(key_of[6], 71), 0),
    }


DECAY = 0.99
EPSILON = 1e-06

def reference(gradient, left_stat, right_stat, left_root, right_root, block_owner):
    position = jnp.arange(NB, dtype=jnp.int32)
    earlier = (block_owner[None, :] == block_owner[:, None]) & (position[None, :] < position[:, None])
    target = (block_owner * SLOTS + lax.optimization_barrier(jnp.sum(earlier.astype(jnp.int32), axis=1))).astype(jnp.int32)
    start_left = DECAY * left_stat
    start_right = DECAY * right_stat

    def update_block(carry, index_now):
        stat_left, stat_right = carry
        slot_now = target[index_now]
        grad_block = lax.dynamic_index_in_dim(gradient, index_now, 0, keepdims=False)
        left_term = jnp.dot(grad_block, grad_block.T, preferred_element_type=jnp.float32)
        right_term = jnp.dot(grad_block.T, grad_block, preferred_element_type=jnp.float32)
        old_left = lax.dynamic_index_in_dim(stat_left, slot_now, 0, keepdims=False)
        old_right = lax.dynamic_index_in_dim(stat_right, slot_now, 0, keepdims=False)
        stat_left = lax.dynamic_update_index_in_dim(stat_left, old_left + (1.0 - DECAY) * left_term, slot_now, 0)
        stat_right = lax.dynamic_update_index_in_dim(stat_right, old_right + (1.0 - DECAY) * right_term, slot_now, 0)
        root_left = lax.dynamic_index_in_dim(left_root, slot_now, 0, keepdims=False)
        root_right = lax.dynamic_index_in_dim(right_root, slot_now, 0, keepdims=False)
        left_part = jnp.dot(root_left, grad_block, preferred_element_type=jnp.float32).astype(jnp.bfloat16)
        raw_update = jnp.dot(left_part, root_right, preferred_element_type=jnp.float32)
        grad_wide = grad_block.astype(jnp.float32)
        graft = jnp.sqrt((jnp.sum(grad_wide * grad_wide) + EPSILON) / (jnp.sum(raw_update * raw_update) + EPSILON))
        return ((stat_left, stat_right), (raw_update * graft).astype(jnp.bfloat16))
    (new_left, new_right), update = lax.scan(update_block, (start_left, start_right), position)
    return (new_left, new_right, update)
```

```python
import jax
import jax.numpy as jnp
from jax import lax
from jax.experimental import pallas as pl
from jax.experimental.pallas import tpu as pltpu
from jax.sharding import PartitionSpec as P

DECAY = 0.99
EPSILON = 1e-06
BF16 = jnp.bfloat16
F32 = jnp.float32
VMEM_SPEC = pl.BlockSpec(memory_space=pltpu.VMEM)
SMEM_SPEC = pl.BlockSpec(memory_space=pltpu.SMEM)
PARAMS = pltpu.CompilerParams(vmem_limit_bytes=48 * 1024 * 1024)


def dot(a, b, ca=1, cb=0):
    return lax.dot_general(a, b, (((ca,), (cb,)), ((), ())), preferred_element_type=F32)


def cost(flops, nbytes):
    return pl.CostEstimate(flops=flops, bytes_accessed=nbytes, transcendentals=0)


def clear_counts(count_ref, owners):
    def clear(i, _):
        count_ref[i] = 0
        return 0

    lax.fori_loop(0, owners, clear, 0)


def route_kernel(owner_ref, grad_ref, first_ref, second_ref, count_ref):
    first_ref[...] = jnp.zeros_like(first_ref)
    second_ref[...] = jnp.zeros_like(second_ref)
    clear_counts(count_ref, first_ref.shape[0])

    def body(b, _):
        o = owner_ref[b]
        c = count_ref[o]
        count_ref[o] = c + 1

        @pl.when(c == 0)
        def _():
            first_ref[o] = grad_ref[b]

        @pl.when(c == 1)
        def _():
            second_ref[o] = grad_ref[b]

        return 0

    lax.fori_loop(0, grad_ref.shape[0], body, 0)


def route(block_owner, gradient, owners):
    _, rows, cols = gradient.shape
    shape = jax.ShapeDtypeStruct((owners, rows, cols), gradient.dtype)
    return pl.pallas_call(
        route_kernel,
        out_shape=(shape, shape),
        in_specs=[SMEM_SPEC, VMEM_SPEC],
        out_specs=(VMEM_SPEC, VMEM_SPEC),
        scratch_shapes=[pltpu.SMEM((owners,), jnp.int32)],
        compiler_params=PARAMS,
        cost_estimate=cost(0, 3 * gradient.size),
        name="route",
    )(block_owner, gradient)


def collect_kernel(owner_ref, first_ref, second_ref, out_ref, count_ref):
    clear_counts(count_ref, first_ref.shape[0])

    def body(b, _):
        o = owner_ref[b]
        c = count_ref[o]
        count_ref[o] = c + 1

        @pl.when(c == 0)
        def _():
            out_ref[b] = first_ref[o]

        @pl.when(c == 1)
        def _():
            out_ref[b] = second_ref[o]

        return 0

    lax.fori_loop(0, out_ref.shape[0], body, 0)


def collect(block_owner, first, second):
    blocks = block_owner.shape[0]
    return pl.pallas_call(
        collect_kernel,
        out_shape=jax.ShapeDtypeStruct((blocks,) + first.shape[1:], first.dtype),
        in_specs=[SMEM_SPEC, VMEM_SPEC, VMEM_SPEC],
        out_specs=VMEM_SPEC,
        scratch_shapes=[pltpu.SMEM((first.shape[0],), jnp.int32)],
        compiler_params=PARAMS,
        cost_estimate=cost(0, 3 * first.size),
        name="collect",
    )(block_owner, first, second)


def three_parts(value):
    high = value.astype(BF16)
    rest = value - high.astype(F32)
    middle = rest.astype(BF16)
    low = (rest - middle.astype(F32)).astype(BF16)
    return high, middle, low


def update_kernel(
    t_ref, l_ref, g0, g1, g3, g2a, g2b, r0, r1, r3, r2a, r2b, o0, o1, o2, o3, raw_ref
):
    width = g0.shape[1]
    left = l_ref[...]
    half = g2a.shape[0]

    def part(g):
        return dot(left, g[...]).astype(BF16)

    raw = dot(part(g0), r0[...])
    raw += dot(part(g1), r1[...])
    raw += dot(part(g3), r3[...])
    far = (dot(left[:, :half], g2a[...]) + dot(left[:, half:], g2b[...])).astype(BF16)
    raw += dot(far[:, : width // 2], r2a[...]) + dot(far[:, width // 2 :], r2b[...])
    raw_ref[...] = raw
    grad_own = g0[...].astype(F32)
    shape = (16, width)
    update_square = jnp.broadcast_to(jnp.sum(raw * raw, keepdims=True), shape)
    grad_square = jnp.broadcast_to(jnp.sum(grad_own * grad_own, keepdims=True), shape)
    row = lax.broadcasted_iota(jnp.int32, shape, 0)
    tile = jnp.zeros(shape, F32)
    for place, value in enumerate(three_parts(update_square) + three_parts(grad_square)):
        tile = jnp.where(row == place, value.astype(F32), tile)
    tile = tile.astype(BF16)
    rows = left.shape[0]
    for k, out in enumerate((o0, o1, o2, o3)):
        s = lax.rem(t_ref[0] + k, 4)
        out[0:rows, :] = raw_ref[:, pl.ds(pl.multiple_of(s * width, width), width)].astype(BF16)
        out[rows : rows + 16, :] = tile


def update_rows(slot, t, left_root, grads, roots):
    g0, g1, g3, g2a, g2b = grads
    r0, r1, r3, r2a, r2b = roots
    _, rows, full = left_root.shape
    width = g0.shape[1]
    slot_spec = pl.BlockSpec((None, rows, full), lambda i: (slot, 0, 0))
    out = jax.ShapeDtypeStruct((rows + 16, width), BF16)
    return pl.pallas_call(
        update_kernel,
        grid=(1,),
        out_shape=(out,) * 4,
        in_specs=[SMEM_SPEC, slot_spec] + [VMEM_SPEC] * 5 + [slot_spec] * 3 + [VMEM_SPEC] * 2,
        out_specs=(VMEM_SPEC,) * 4,
        scratch_shapes=[pltpu.VMEM((rows, full), F32)],
        compiler_params=PARAMS,
        cost_estimate=cost(4 * rows * full * full, 10 * rows * full * 2),
        name="update_rows",
    )(t, left_root, g0, g1, g3, g2a, g2b, r0, r1, r3, r2a, r2b)


def scale_kernel(t_ref, q0, q1, q2, q3, out_ref):
    rows = q0.shape[0] - 16

    def total(q, first):
        part = q[rows : rows + 16, 0:1].astype(F32)
        return part[first : first + 1] + part[first + 1 : first + 2] + part[first + 2 : first + 3]

    update_square = total(q0, 0) + total(q1, 0) + total(q2, 0) + total(q3, 0)
    grad_square = total(q0, 3) + total(q1, 3) + total(q2, 3) + total(q3, 3)
    graft = jnp.sqrt((grad_square + EPSILON) / (update_square + EPSILON))
    for k, q in enumerate((q0, q1, q2, q3)):
        s = lax.rem(t_ref[0] + 4 - k, 4)
        scaled = (q[0:rows, :].astype(F32) * graft).astype(BF16)
        out_ref[pl.ds(pl.multiple_of(s * rows, rows), rows), :] = scaled


def scale(t, pieces):
    rows, width = pieces[0].shape
    return pl.pallas_call(
        scale_kernel,
        out_shape=jax.ShapeDtypeStruct((4 * (rows - 16), width), BF16),
        in_specs=[SMEM_SPEC] + [VMEM_SPEC] * 4,
        out_specs=VMEM_SPEC,
        compiler_params=PARAMS,
        cost_estimate=cost(0, 16 * rows * width),
        name="scale",
    )(t, *pieces)


def stats_kernel(t_ref, *refs):
    slot_grads = (refs[0:5], refs[5:10])
    left_ref, right_ref, new_left_ref, new_right_ref = refs[10:]
    t = t_ref[0]
    rows = left_ref.shape[0]

    def work(g0, g1, g3, g2a, g2b):
        mine = pl.ds(pl.multiple_of(t * rows, rows), rows)
        half = g2a.shape[0]
        term = dot(g0[mine, :], g0[...], 1, 1)
        term += dot(g1[mine, :], g1[...], 1, 1)
        term += dot(g3[mine, :], g3[...], 1, 1)
        new_left_ref[...] = DECAY * left_ref[...] + (1.0 - DECAY) * term

        def far(g, other):
            inside = pl.ds(pl.multiple_of(lax.rem(t, 2) * rows, rows), rows)
            top = g[inside, :]
            new_left_ref[:, 0:half] += (1.0 - DECAY) * dot(top, g2a[...], 1, 1)
            new_left_ref[:, half:] += (1.0 - DECAY) * dot(top, g2b[...], 1, 1)

        pl.when(t < 2)(lambda: far(g2a, g2b))
        pl.when(t >= 2)(lambda: far(g2b, g2a))
        own = g0[...].T

        def place(k, term):
            s = lax.rem(t + 4 - k, 4)
            cols = pl.ds(pl.multiple_of(s * rows, rows), rows)
            new_right_ref[:, cols] = DECAY * right_ref[:, cols] + (1.0 - DECAY) * term

        place(0, dot(own, g0[...]))
        place(1, dot(own, g1[...]))
        place(3, dot(own, g3[...]))
        place(2, dot(own[:, :half], g2a[...]) + dot(own[:, half:], g2b[...]))

    for slot in range(2):
        pl.when(pl.program_id(0) == slot)(lambda: work(*slot_grads[slot]))


def statistics(t, grads_first, grads_second, left_stat, right_stat):
    slots, rows, full = left_stat.shape
    slot_spec = pl.BlockSpec((None, rows, full), lambda i: (i, 0, 0))
    shape = jax.ShapeDtypeStruct(left_stat.shape, F32)
    return pl.pallas_call(
        stats_kernel,
        grid=(slots,),
        out_shape=(shape, shape),
        in_specs=[SMEM_SPEC] + [VMEM_SPEC] * 10 + [slot_spec] * 2,
        out_specs=(slot_spec, slot_spec),
        compiler_params=PARAMS,
        cost_estimate=cost(8 * rows * full * full, 24 * rows * full),
        name="statistics",
    )(t, *grads_first, *grads_second, left_stat, right_stat)


def around(x, k):
    n = lax.axis_size("tensor")
    return lax.ppermute(x, "tensor", [(i, (i + k) % n) for i in range(n)])


def gather_ring(x):
    half = x.shape[0] // 2
    below, above = around(x, 1), around(x, -1)
    return x, below, above, around(below[:half], 1), around(above[half:], -1)


def on_device(gradient, left_stat, right_stat, left_root, right_root, block_owner):
    owners = lax.axis_size("fsdp")
    t = lax.axis_index("tensor").reshape(1)
    cols = gradient.shape[2]

    def exchange(x):
        return lax.all_to_all(x, "fsdp", split_axis=0, concat_axis=0, tiled=True)

    root_below, root_above = around(right_root, 1), around(right_root, -1)

    def root_far(slot):
        half = right_root.shape[1] // 2
        return around(root_below[slot, :half], 1), around(root_above[slot, half:], -1)

    routed = route(block_owner, gradient, owners)
    grads, returned = [], []
    for slot in range(2):
        grads.append(gather_ring(exchange(routed[slot]).reshape(-1, cols)))
        roots = (right_root, root_below, root_above) + root_far(slot)
        pieces = update_rows(slot, t, left_root, grads[slot], roots)
        arrived = [pieces[0]] + [around(pieces[k], k) for k in (1, 2, 3)]
        returned.append(exchange(scale(t, arrived).reshape(owners, -1, cols)))
    new_left, new_right = statistics(t, grads[0], grads[1], left_stat, right_stat)
    return (new_left, new_right, collect(block_owner, *returned))


def solution(mesh):
    return jax.shard_map(
        on_device,
        mesh=mesh,
        in_specs=(
            P(None, "fsdp", "tensor"),
            P("fsdp", "tensor", None),
            P("fsdp", "tensor", None),
            P("fsdp", "tensor", None),
            P("fsdp", "tensor", None),
            P(),
        ),
        out_specs=(P("fsdp", "tensor", None), P("fsdp", "tensor", None), P(None, "fsdp", "tensor")),
        check_vma=False,
    )
```

```python
import functools

import jax
import jax.numpy as jnp
from jax import lax
from jax.experimental import pallas as pl
from jax.experimental.pallas import tpu as pltpu
from jax.sharding import PartitionSpec as P

DECAY = 0.99
EPSILON = 1e-06
BF16 = jnp.bfloat16
F32 = jnp.float32
VMEM_SPEC = pl.BlockSpec(memory_space=pltpu.VMEM)
SMEM_SPEC = pl.BlockSpec(memory_space=pltpu.SMEM)
ANY_SPEC = pl.BlockSpec(memory_space=pl.ANY)
PARAMS = pltpu.CompilerParams(vmem_limit_bytes=48 * 1024 * 1024)


def dot(a, b, ca=1, cb=0):
    return lax.dot_general(a, b, (((ca,), (cb,)), ((), ())), preferred_element_type=F32)


def cost(flops, nbytes):
    return pl.CostEstimate(flops=flops, bytes_accessed=nbytes, transcendentals=0)


def clear_counts(count_ref, owners):
    def clear(i, _):
        count_ref[i] = 0
        return 0

    lax.fori_loop(0, owners, clear, 0, unroll=8)


def route_kernel(owner_ref, grad_hbm, out_hbm, grad, out, count_ref, sems):
    bring = pltpu.make_async_copy(grad_hbm, grad, sems.at[0])
    bring.start()
    out[...] = jnp.zeros_like(out)
    clear_counts(count_ref, out.shape[0])
    bring.wait()

    def body(b, _):
        o = owner_ref[b]
        c = count_ref[o]
        count_ref[o] = c + 1
        out[o, c] = grad[b]
        return 0

    lax.fori_loop(0, grad.shape[0], body, 0, unroll=8)
    send = pltpu.make_async_copy(out, out_hbm, sems.at[1])
    send.start()
    send.wait()


def route(block_owner, gradient, owners):
    _, rows, cols = gradient.shape
    shape = (owners, 2, rows, cols)
    return pl.pallas_call(
        route_kernel,
        out_shape=jax.ShapeDtypeStruct(shape, gradient.dtype),
        in_specs=[SMEM_SPEC, ANY_SPEC],
        out_specs=ANY_SPEC,
        scratch_shapes=[
            pltpu.VMEM(gradient.shape, gradient.dtype),
            pltpu.VMEM(shape, gradient.dtype),
            pltpu.SMEM((owners,), jnp.int32),
            pltpu.SemaphoreType.DMA((2,)),
        ],
        compiler_params=PARAMS,
        cost_estimate=cost(0, 3 * gradient.size),
        name="route",
    )(block_owner, gradient)


def collect_kernel(owner_ref, slots_hbm, out_hbm, slots, out, count_ref, sems):
    bring = pltpu.make_async_copy(slots_hbm, slots, sems.at[0])
    bring.start()
    clear_counts(count_ref, slots.shape[0])
    bring.wait()

    def body(b, _):
        o = owner_ref[b]
        c = count_ref[o]
        count_ref[o] = c + 1
        out[b] = slots[o, c]
        return 0

    lax.fori_loop(0, out.shape[0], body, 0, unroll=8)
    send = pltpu.make_async_copy(out, out_hbm, sems.at[1])
    send.start()
    send.wait()


def collect(block_owner, slots):
    shape = (block_owner.shape[0],) + slots.shape[2:]
    return pl.pallas_call(
        collect_kernel,
        out_shape=jax.ShapeDtypeStruct(shape, slots.dtype),
        in_specs=[SMEM_SPEC, ANY_SPEC],
        out_specs=ANY_SPEC,
        scratch_shapes=[
            pltpu.VMEM(slots.shape, slots.dtype),
            pltpu.VMEM(shape, slots.dtype),
            pltpu.SMEM((slots.shape[0],), jnp.int32),
            pltpu.SemaphoreType.DMA((2,)),
        ],
        compiler_params=PARAMS,
        cost_estimate=cost(0, 3 * slots.size),
        name="collect",
    )(block_owner, slots)


def split_kernel(both_hbm, first_hbm, second_hbm, sems):
    copies = [
        pltpu.make_async_copy(both_hbm.at[:, slot], out, sems.at[slot])
        for slot, out in enumerate((first_hbm, second_hbm))
    ]
    for c in copies:
        c.start()
    for c in copies:
        c.wait()


def split(both):
    shape = jax.ShapeDtypeStruct((both.shape[0],) + both.shape[2:], both.dtype)
    return pl.pallas_call(
        split_kernel,
        out_shape=(shape, shape),
        in_specs=[ANY_SPEC],
        out_specs=(ANY_SPEC, ANY_SPEC),
        scratch_shapes=[pltpu.SemaphoreType.DMA((2,))],
        compiler_params=PARAMS,
        cost_estimate=cost(0, 4 * both.size),
        name="split",
    )(both)


def three_parts(value):
    high = value.astype(BF16)
    rest = value - high.astype(F32)
    middle = rest.astype(BF16)
    low = (rest - middle.astype(F32)).astype(BF16)
    return high, middle, low


def pick_kernel(first, second, below_hbm, above_hbm, first_hbm, second_hbm, sems):
    copies = [
        pltpu.make_async_copy(below_hbm.at[first], first_hbm, sems.at[0]),
        pltpu.make_async_copy(above_hbm.at[second], second_hbm, sems.at[1]),
    ]
    for c in copies:
        c.start()
    for c in copies:
        c.wait()


def pick(below, above, first, second, shape, flops):
    shape = jax.ShapeDtypeStruct(shape, below.dtype)
    return pl.pallas_call(
        functools.partial(pick_kernel, first, second),
        out_shape=(shape, shape),
        in_specs=[ANY_SPEC] * 2,
        out_specs=(ANY_SPEC, ANY_SPEC),
        scratch_shapes=[pltpu.SemaphoreType.DMA((2,))],
        compiler_params=PARAMS,
        cost_estimate=cost(flops, 4 * below.size),
        name="pick",
    )(below, above)


def opposite(below, above):
    rows, width = below.shape
    half = rows // 2
    upper, lower = pick(below, above, pl.ds(0, half), pl.ds(half, half), (half, width), 3 * 10**10)
    return around(upper, 1), around(lower, -1)


def update_kernel(
    slot, t_ref, l_hbm, g0, g1, g3, g2a, g2b, r0, r1, r3, r2, o0, o1, o2, o3, left, grads, roots, raw_ref, sems
):
    bring = [pltpu.make_async_copy(l_hbm.at[slot], left, sems.at[8])]
    for i, (g, r) in enumerate(((g0, r0), (g1, r1), (g3, r3), (g2a, r2))):
        r = r.at[slot] if i < 3 else r
        to = grads.at[i] if i < 3 else grads.at[3, pl.ds(0, g2a.shape[0])]
        bring.append(pltpu.make_async_copy(g, to, sems.at[2 * i]))
        bring.append(pltpu.make_async_copy(r, roots.at[i], sems.at[2 * i + 1]))
    lower = grads.at[3, pl.ds(g2a.shape[0], g2b.shape[0])]
    bring.append(pltpu.make_async_copy(g2b, lower, sems.at[9]))
    for c in bring:
        c.start()
    rows = left.shape[0]
    width = o0.shape[1]
    bring[0].wait()
    raw = None
    for i in range(4):
        bring[2 * i + 1].wait()
        if i == 3:
            bring[9].wait()
        part = dot(left[...], grads[i]).astype(BF16)
        bring[2 * i + 2].wait()
        term = dot(part, roots[i])
        raw = term if raw is None else raw + term
    raw_ref[...] = raw
    grad_own = grads[0].astype(F32)
    shape = (16, width)
    update_square = jnp.broadcast_to(jnp.sum(raw * raw, keepdims=True), shape)
    grad_square = jnp.broadcast_to(jnp.sum(grad_own * grad_own, keepdims=True), shape)
    row = lax.broadcasted_iota(jnp.int32, shape, 0)
    tile = jnp.zeros(shape, F32)
    for place, value in enumerate(three_parts(update_square) + three_parts(grad_square)):
        tile = jnp.where(row == place, value.astype(F32), tile)
    for k, out in enumerate((o0, o1, o2, o3)):
        s = lax.rem(t_ref[0] + k, 4)
        cols = pl.ds(pl.multiple_of(s * width, width), width)
        out[0:rows, :] = raw_ref[:, cols].astype(BF16)
        out[rows : rows + 16, :] = tile.astype(BF16)


def update_rows(slot, t, left_root, grads, roots):
    _, rows, full = left_root.shape
    width = grads[0].shape[1]
    out = jax.ShapeDtypeStruct((rows + 16, width), BF16)
    return pl.pallas_call(
        functools.partial(update_kernel, slot),
        out_shape=(out,) * 4,
        in_specs=[SMEM_SPEC] + [ANY_SPEC] * 10,
        out_specs=(VMEM_SPEC,) * 4,
        scratch_shapes=[
            pltpu.VMEM((rows, full), BF16),
            pltpu.VMEM((4, full, width), BF16),
            pltpu.VMEM((4, rows, full), BF16),
            pltpu.VMEM((rows, full), F32),
            pltpu.SemaphoreType.DMA((10,)),
        ],
        compiler_params=PARAMS,
        cost_estimate=cost(4 * rows * full * full, 10 * rows * full * 2),
        name="update_rows",
    )(t, left_root, *grads, *roots)


def scale_kernel(t_ref, *refs):
    slot_pieces = (refs[0:4], refs[4:8])
    out_hbm, ready, sems = refs[8:]
    _, here, _, height, width = ready.shape
    rows = here * height
    grafts = []
    for pieces in slot_pieces:
        tiles = [q[rows : rows + 16, 0:1].astype(F32) for q in pieces]

        def total(first):
            parts = [x[first : first + 1] + x[first + 1 : first + 2] + x[first + 2 : first + 3] for x in tiles]
            return parts[0] + parts[1] + parts[2] + parts[3]

        grafts.append(jnp.sqrt((total(3) + EPSILON) / (total(0) + EPSILON)))
    copies = []
    for k in range(4):
        for slot, pieces in enumerate(slot_pieces):
            scaled = pieces[k][0:rows, :].astype(F32) * grafts[slot]
            ready[k, :, slot] = scaled.astype(BF16).reshape(here, height, width)
        s = lax.rem(t_ref[0] + 4 - k, 4)
        to = out_hbm.at[pl.ds(s * here, here)]
        copies.append(pltpu.make_async_copy(ready.at[k], to, sems.at[k]))
        copies[k].start()
    for c in copies:
        c.wait()


def scale(t, first, second, shape):
    owners, slots, height, width = shape
    return pl.pallas_call(
        scale_kernel,
        out_shape=jax.ShapeDtypeStruct(shape, BF16),
        in_specs=[SMEM_SPEC] + [VMEM_SPEC] * 8,
        out_specs=ANY_SPEC,
        scratch_shapes=[
            pltpu.VMEM((4, owners // 4, slots, height, width), BF16),
            pltpu.SemaphoreType.DMA((4,)),
        ],
        compiler_params=PARAMS,
        cost_estimate=cost(0, 16 * owners * height * width),
        name="scale",
    )(t, *first, *second)


def stats_kernel(t_ref, *refs):
    slot_grads = (refs[0:3], refs[3:6])
    halves = refs[6:10]
    left_ref, right_ref, new_left_ref, new_right_ref, far, sems = refs[10:]
    t = t_ref[0]
    rows = left_ref.shape[0]
    mine = pl.ds(pl.multiple_of(t * rows, rows), rows)

    def work(slot):
        half = halves[0].shape[0]
        copies = []
        for i in range(2):
            to = far.at[slot, pl.ds(i * half, half)]
            copies.append(pltpu.make_async_copy(halves[2 * slot + i], to, sems.at[slot, i]))
        for c in copies:
            c.start()
        grads = slot_grads[slot]
        own = grads[0][...].T

        def place(k, g):
            s = lax.rem(t + 4 - k, 4)
            cols = pl.ds(pl.multiple_of(s * rows, rows), rows)
            new_right_ref[:, cols] = DECAY * right_ref[:, cols] + (1.0 - DECAY) * dot(own, g[...])

        term = None
        for k, g in zip((0, 1, 3), grads):
            part = dot(g[mine, :], g[...], 1, 1)
            term = part if term is None else term + part
            place(k, g)
        for c in copies:
            c.wait()
        term += dot(far[slot, mine, :], far[slot], 1, 1)
        place(2, far.at[slot])
        new_left_ref[...] = DECAY * left_ref[...] + (1.0 - DECAY) * term

    for slot in range(2):
        pl.when(pl.program_id(0) == slot)(lambda: work(slot))


def statistics(t, first, second, left_stat, right_stat):
    slots, rows, full = left_stat.shape
    slot_spec = pl.BlockSpec((None, rows, full), lambda i: (i, 0, 0))
    shape = jax.ShapeDtypeStruct(left_stat.shape, F32)
    return pl.pallas_call(
        stats_kernel,
        grid=(slots,),
        out_shape=(shape, shape),
        in_specs=[SMEM_SPEC] + [VMEM_SPEC] * 6 + [ANY_SPEC] * 4 + [slot_spec] * 2,
        out_specs=(slot_spec, slot_spec),
        scratch_shapes=[
            pltpu.VMEM((slots, full, first[0].shape[1]), BF16),
            pltpu.SemaphoreType.DMA((slots, 2)),
        ],
        compiler_params=PARAMS,
        cost_estimate=cost(8 * rows * full * full, 24 * rows * full),
        name="statistics",
    )(t, *first[:3], *second[:3], *first[3:], *second[3:], left_stat, right_stat)


def around(x, k):
    n = lax.axis_size("tensor")
    return lax.ppermute(x, "tensor", [(i, (i + k) % n) for i in range(n)])


def exchange(x):
    return lax.all_to_all(x, "fsdp", split_axis=0, concat_axis=0, tiled=True)


def on_device(gradient, left_stat, right_stat, left_root, right_root, block_owner):
    owners = lax.axis_size("fsdp")
    t = lax.axis_index("tensor").reshape(1)
    cols = gradient.shape[2]
    root_below, root_above = around(right_root, 1), around(right_root, -1)
    onward = pick(root_below, root_above, 0, 1, right_root.shape[1:], 2 * 10**11)
    root_far = [around(onward[0], 1), around(onward[1], -1)]
    routed = route(block_owner, gradient, owners)
    owned = exchange(routed)
    owned, root_far = lax.optimization_barrier((owned, root_far))
    own_0, own_1 = (x.reshape(-1, cols) for x in split(owned))
    grads = []
    for own in (own_0, own_1):
        below, above = around(own, 1), around(own, -1)
        grads.append((own, below, above) + opposite(below, above))
    arrived = []
    for slot in range(2):
        roots = (right_root, root_below, root_above, root_far[slot])
        pieces = update_rows(slot, t, left_root, grads[slot], roots)
        if slot == 1:
            pieces, arrived[0] = lax.optimization_barrier((pieces, arrived[0]))
        arrived.append([pieces[0]] + [around(pieces[k], k) for k in (1, 2, 3)])
    returned = exchange(scale(t, *arrived, routed.shape))
    new_left, new_right = statistics(t, *grads, left_stat, right_stat)
    return (new_left, new_right, collect(block_owner, returned))


def solution(mesh):
    return jax.shard_map(
        on_device,
        mesh=mesh,
        in_specs=(
            P(None, "fsdp", "tensor"),
            P("fsdp", "tensor", None),
            P("fsdp", "tensor", None),
            P("fsdp", "tensor", None),
            P("fsdp", "tensor", None),
            P(),
        ),
        out_specs=(P("fsdp", "tensor", None), P("fsdp", "tensor", None), P(None, "fsdp", "tensor")),
        check_vma=False,
    )
```

```python
import functools

import jax
import jax.numpy as jnp
from jax import lax
from jax.experimental import pallas as pl
from jax.experimental.pallas import tpu as pltpu
from jax.sharding import PartitionSpec as P

DECAY = 0.99
EPSILON = 1e-06
BF16 = jnp.bfloat16
F32 = jnp.float32
VMEM_SPEC = pl.BlockSpec(memory_space=pltpu.VMEM)
SMEM_SPEC = pl.BlockSpec(memory_space=pltpu.SMEM)
HBM_SPEC = pl.BlockSpec(memory_space=pltpu.HBM)
PARAMS = pltpu.CompilerParams(vmem_limit_bytes=20 * 1024 * 1024)
WHOLE = pltpu.CompilerParams(vmem_limit_bytes=63 * 1024 * 1024)


def dot(a, b, ca=1, cb=0):
    return lax.dot_general(a, b, (((ca,), (cb,)), ((), ())), preferred_element_type=F32)


def cost(flops, nbytes):
    return pl.CostEstimate(flops=flops, bytes_accessed=nbytes, transcendentals=0)


def clear_counts(count_ref, owners):
    def clear(i, _):
        count_ref[i] = 0
        return 0

    lax.fori_loop(0, owners, clear, 0, unroll=8)


def route_kernel(
    t_ref, owner_hbm, grad_hbm, root_hbm, out_hbm, c1, c2, c3, grad, out, root, owner_ref, count_ref, sems
):
    bring = [
        pltpu.make_async_copy(owner_hbm, owner_ref, sems.at[0]),
        pltpu.make_async_copy(grad_hbm, grad, sems.at[1]),
        pltpu.make_async_copy(root_hbm, root, sems.at[2]),
    ]
    for c in bring:
        c.start()
    out[...] = jnp.zeros_like(out)
    clear_counts(count_ref, out.shape[0])
    bring[0].wait()
    bring[1].wait()

    def body(b, _):
        o = owner_ref[b]
        c = count_ref[o]
        count_ref[o] = c + 1
        out[o, c] = grad[b]
        return 0

    lax.fori_loop(0, grad.shape[0], body, 0, unroll=8)
    sends = [pltpu.make_async_copy(out, out_hbm, sems.at[3])]
    sends[0].start()
    bring[2].wait()
    width = c1.shape[2]
    for k, c in ((1, c1), (2, c2), (3, c3)):
        s = lax.rem(t_ref[0] + k, 4)
        cols = root.at[:, :, pl.ds(pl.multiple_of(s * width, width), width)]
        sends.append(pltpu.make_async_copy(cols, c, sems.at[3 + k]))
        sends[k].start()
    for c in sends:
        c.wait()


def route(t, block_owner, gradient, right_root, owners):
    blocks, rows, cols = gradient.shape
    shape = (owners, 2, rows, cols)
    cut = jax.ShapeDtypeStruct(right_root.shape[:2] + (cols,), right_root.dtype)
    return pl.pallas_call(
        route_kernel,
        out_shape=(jax.ShapeDtypeStruct(shape, gradient.dtype), cut, cut, cut),
        in_specs=[SMEM_SPEC] + [HBM_SPEC] * 3,
        out_specs=(HBM_SPEC,) * 4,
        scratch_shapes=[
            pltpu.VMEM(gradient.shape, gradient.dtype),
            pltpu.VMEM(shape, gradient.dtype),
            pltpu.VMEM(right_root.shape, right_root.dtype),
            pltpu.SMEM((blocks,), jnp.int32),
            pltpu.SMEM((owners,), jnp.int32),
            pltpu.SemaphoreType.DMA((7,)),
        ],
        compiler_params=WHOLE,
        cost_estimate=cost(0, 3 * gradient.size),
        name="route",
    )(t, block_owner, gradient, right_root)


def collect_kernel(owner_hbm, slots_hbm, out_hbm, slots, out, owner_ref, count_ref, sems):
    bring = [
        pltpu.make_async_copy(owner_hbm, owner_ref, sems.at[0]),
        pltpu.make_async_copy(slots_hbm, slots, sems.at[1]),
    ]
    for c in bring:
        c.start()
    clear_counts(count_ref, slots.shape[0])
    for c in bring:
        c.wait()

    def body(b, _):
        o = owner_ref[b]
        c = count_ref[o]
        count_ref[o] = c + 1
        out[b] = slots[o, c]
        return 0

    lax.fori_loop(0, out.shape[0], body, 0, unroll=8)
    send = pltpu.make_async_copy(out, out_hbm, sems.at[2])
    send.start()
    send.wait()


def collect(block_owner, slots):
    blocks = block_owner.shape[0]
    shape = (blocks,) + slots.shape[2:]
    return pl.pallas_call(
        collect_kernel,
        out_shape=jax.ShapeDtypeStruct(shape, slots.dtype),
        in_specs=[HBM_SPEC] * 2,
        out_specs=HBM_SPEC,
        scratch_shapes=[
            pltpu.VMEM(slots.shape, slots.dtype),
            pltpu.VMEM(shape, slots.dtype),
            pltpu.SMEM((blocks,), jnp.int32),
            pltpu.SMEM((slots.shape[0],), jnp.int32),
            pltpu.SemaphoreType.DMA((3,)),
        ],
        compiler_params=PARAMS,
        cost_estimate=cost(0, 3 * slots.size),
        name="collect",
    )(block_owner, slots)


def through(brings, sends):
    for c in brings:
        c.start()
    for bring, send in zip(brings, sends):
        bring.wait()
        send.start()
    for c in sends:
        c.wait()


def pick_kernel(first, second, below_hbm, above_hbm, first_hbm, second_hbm, held, sems):
    brings = [
        pltpu.make_async_copy(below_hbm.at[first], held.at[0], sems.at[0]),
        pltpu.make_async_copy(above_hbm.at[second], held.at[1], sems.at[1]),
    ]
    sends = [
        pltpu.make_async_copy(held.at[i], out, sems.at[2 + i])
        for i, out in enumerate((first_hbm, second_hbm))
    ]
    through(brings, sends)


def pick(below, above, first, second, shape, flops, params):
    out = jax.ShapeDtypeStruct(shape, below.dtype)
    return pl.pallas_call(
        functools.partial(pick_kernel, first, second),
        out_shape=(out, out),
        in_specs=[HBM_SPEC] * 2,
        out_specs=(HBM_SPEC, HBM_SPEC),
        scratch_shapes=[pltpu.VMEM((2,) + shape, below.dtype), pltpu.SemaphoreType.DMA((4,))],
        compiler_params=params,
        cost_estimate=cost(flops, 4 * below.size),
        name="pick",
    )(below, above)


def bring_left(slot, own, below, above, far, to, sems):
    rows = far.shape[0]
    pieces = (own.at[slot], below.at[slot], above.at[slot], far)
    return [
        pltpu.make_async_copy(x, to.at[pl.ds(i * rows, rows)], sems.at[i])
        for i, x in enumerate(pieces)
    ]


def own_kernel(t_ref, l0, l1, l3, l2_0, l2_1, g0, r0, raw_ref, square_ref, left, grads, roots, sems):
    slots, full, _ = left.shape
    width = grads.shape[3]
    mine = pl.ds(pl.multiple_of(t_ref[0] * width, width), width)
    groups = []
    for slot, far in enumerate((l2_0, l2_1)):
        bring = bring_left(slot, l0, l1, l3, far, left.at[slot], sems.at[slot])
        bring.append(pltpu.make_async_copy(g0.at[:, slot], grads.at[slot], sems.at[slot, 4]))
        bring.append(pltpu.make_async_copy(r0.at[slot, :, mine], roots.at[slot], sems.at[slot, 5]))
        groups.append(bring)
    for bring in groups:
        for c in bring:
            c.start()
    for slot, bring in enumerate(groups):
        for c in bring:
            c.wait()
        grad = grads[slot].reshape(full, width)
        raw_ref[slot] = dot(dot(left[slot], grad).astype(BF16), roots[slot])
        wide = grad.astype(F32)
        square_ref[slot] = jnp.broadcast_to(jnp.sum(wide * wide, keepdims=True), square_ref.shape[1:])


def own_part(t, lefts, lefts_far, owned, right_root):
    owners, slots, height, width = owned.shape
    full = owners * height
    return pl.pallas_call(
        own_kernel,
        out_shape=(
            jax.ShapeDtypeStruct((slots, full, width), F32),
            jax.ShapeDtypeStruct((slots, 8, 128), F32),
            jax.ShapeDtypeStruct((slots, full, full), BF16),
        ),
        in_specs=[SMEM_SPEC] + [HBM_SPEC] * 7,
        out_specs=(VMEM_SPEC,) * 3,
        scratch_shapes=[
            pltpu.VMEM((slots, owners, height, width), BF16),
            pltpu.VMEM((slots, width, width), BF16),
            pltpu.SemaphoreType.DMA((slots, 6)),
        ],
        compiler_params=PARAMS,
        cost_estimate=cost(4 * full * full * width, 12 * full * full),
        name="own_part",
    )(t, *lefts, *lefts_far, owned, right_root)


def near_kernel(own, left, g1, g3, r1, r3, raw_ref, grads, roots, sems):
    slots, full, _ = left.shape
    width = grads.shape[4]
    groups = []
    for slot in range(slots):
        bring = []
        for i, (g, r) in enumerate(((g1, r1), (g3, r3))):
            bring.append(pltpu.make_async_copy(g.at[:, slot], grads.at[slot, i], sems.at[slot, 2 * i]))
            bring.append(pltpu.make_async_copy(r.at[slot], roots.at[slot, i], sems.at[slot, 2 * i + 1]))
        groups.append(bring)
    for bring in groups:
        for c in bring:
            c.start()
    for slot, bring in enumerate(groups):
        raw = own[slot]
        for i in range(2):
            bring[2 * i].wait()
            bring[2 * i + 1].wait()
            part = dot(left[slot], grads[slot, i].reshape(full, width)).astype(BF16)
            raw = raw + dot(part, roots[slot, i])
        raw_ref[slot] = raw


def near_part(own, left, below, above, root_below, root_above):
    owners, slots, height, width = below.shape
    return pl.pallas_call(
        near_kernel,
        out_shape=jax.ShapeDtypeStruct(own.shape, F32),
        in_specs=[VMEM_SPEC] * 2 + [HBM_SPEC] * 4,
        out_specs=VMEM_SPEC,
        scratch_shapes=[
            pltpu.VMEM((slots, 2, owners, height, width), BF16),
            pltpu.VMEM((slots, 2, width, width), BF16),
            pltpu.SemaphoreType.DMA((slots, 4)),
        ],
        compiler_params=PARAMS,
        cost_estimate=cost(8 * own.shape[1] ** 2 * width, 12 * own.shape[1] ** 2),
        name="near_part",
    )(own, left, below, above, root_below, root_above)


def far_kernel(near, square, left, ga, gb, r2, raw_ref, sums_ref):
    row = lax.broadcasted_iota(jnp.int32, sums_ref.shape, 0)
    sums = jnp.zeros(sums_ref.shape, F32)
    half = left.shape[1] // 2
    width = near.shape[2]
    for slot in range(near.shape[0]):
        part = dot(left[slot, :, :half], ga[:, slot].reshape(half, width))
        part += dot(left[slot, :, half:], gb[:, slot].reshape(half, width))
        total = near[slot] + dot(part.astype(BF16), r2[slot])
        raw_ref[slot] = total
        sums = jnp.where(row == slot, jnp.sum(total * total, keepdims=True), sums)
        sums = jnp.where(row == 2 + slot, square[slot], sums)
    sums_ref[...] = sums


def far_part(near, square, left, halves, root_far):
    slots, full, width = near.shape
    return pl.pallas_call(
        far_kernel,
        out_shape=(
            jax.ShapeDtypeStruct(near.shape, F32),
            jax.ShapeDtypeStruct((8, 128), F32),
        ),
        in_specs=[VMEM_SPEC] * 6,
        out_specs=(VMEM_SPEC, VMEM_SPEC),
        compiler_params=PARAMS,
        cost_estimate=cost(4 * full * full * width, 8 * full * full),
        name="far_part",
    )(near, square, left, *halves, root_far)


def scale_kernel(t_ref, raw, s0, s1, s2, s3, out_hbm, ready, sems):
    _, here, slots, height, width = ready.shape
    rows = here * height
    sums = s0[...] + s1[...] + s2[...] + s3[...]
    grafts = [
        jnp.sqrt((sums[2 + slot : 3 + slot, 0:1] + EPSILON) / (sums[slot : slot + 1, 0:1] + EPSILON))
        for slot in range(slots)
    ]
    copies = []
    for i, k in enumerate((0, 1, 3, 2)):
        for slot in range(slots):
            scaled = raw[slot, i * rows : (i + 1) * rows, :] * grafts[slot]
            ready[i, :, slot] = scaled.astype(BF16).reshape(here, height, width)
        s = lax.rem(t_ref[0] + 4 - k, 4)
        to = out_hbm.at[pl.ds(s * here, here)]
        copies.append(pltpu.make_async_copy(ready.at[i], to, sems.at[i]))
        copies[i].start()
    for c in copies:
        c.wait()


def scale(t, raw, sums, shape):
    owners, slots, height, width = shape
    return pl.pallas_call(
        scale_kernel,
        out_shape=jax.ShapeDtypeStruct(shape, BF16),
        in_specs=[SMEM_SPEC] + [VMEM_SPEC] * 5,
        out_specs=HBM_SPEC,
        scratch_shapes=[
            pltpu.VMEM((4, owners // 4, slots, height, width), BF16),
            pltpu.SemaphoreType.DMA((4,)),
        ],
        compiler_params=PARAMS,
        cost_estimate=cost(0, 16 * owners * height * width),
        name="scale",
    )(t, raw, *sums)


def stats_kernel(
    t_ref, g0, g1, g3, ga, gb, left_ref, right_ref, new_left_ref, new_right_ref, far, sems
):
    t = t_ref[0]
    rows, full = left_ref.shape
    here = g0.shape[0] // 4
    half = ga.shape[0]
    mine = pl.ds(pl.multiple_of(t * here, here), here)

    def work(slot):
        copies = []
        for i, g in enumerate((ga, gb)):
            to = far.at[slot, pl.ds(i * half, half)]
            copies.append(pltpu.make_async_copy(g.at[:, slot], to, sems.at[slot, i]))
            copies[i].start()

        def place(k, g):
            s = lax.rem(t + 4 - k, 4)
            cols = pl.ds(pl.multiple_of(s * rows, rows), rows)
            new_right_ref[:, cols] = DECAY * right_ref[:, cols] + (1.0 - DECAY) * dot(own, g)

        own = g0[:, slot].reshape(full, rows).T
        term = None
        for k, g in ((0, g0), (1, g1), (3, g3)):
            whole = g[:, slot].reshape(full, rows)
            part = dot(g[mine, slot].reshape(rows, rows), whole, 1, 1)
            term = part if term is None else term + part
            place(k, whole)
        for c in copies:
            c.wait()
        whole = far[slot].reshape(full, rows)
        term += dot(far[slot, mine].reshape(rows, rows), whole, 1, 1)
        place(2, whole)
        new_left_ref[...] = DECAY * left_ref[...] + (1.0 - DECAY) * term

    for slot in range(2):
        pl.when(pl.program_id(0) == slot)(functools.partial(work, slot))


def statistics(t, grads, halves, left_stat, right_stat):
    slots, rows, full = left_stat.shape
    slot_spec = pl.BlockSpec((None, rows, full), lambda i: (i, 0, 0))
    shape = jax.ShapeDtypeStruct(left_stat.shape, F32)
    owners, _, height, width = grads[0].shape
    return pl.pallas_call(
        stats_kernel,
        grid=(slots,),
        out_shape=(shape, shape),
        in_specs=[SMEM_SPEC] + [VMEM_SPEC] * 3 + [HBM_SPEC] * 2 + [slot_spec] * 2,
        out_specs=(slot_spec, slot_spec),
        scratch_shapes=[
            pltpu.VMEM((slots, owners, height, width), BF16),
            pltpu.SemaphoreType.DMA((slots, 2)),
        ],
        compiler_params=pltpu.CompilerParams(vmem_limit_bytes=32 * 1024 * 1024),
        cost_estimate=cost(8 * rows * full * full, 24 * rows * full),
        name="statistics",
    )(t, *grads, *halves, left_stat, right_stat)


def around(x, k):
    n = lax.axis_size("tensor")
    return lax.ppermute(x, "tensor", [(i, (i + k) % n) for i in range(n)])


def exchange(x):
    return lax.all_to_all(x, "fsdp", split_axis=0, concat_axis=0, tiled=True)


def on_device(gradient, left_stat, right_stat, left_root, right_root, block_owner):
    owners = lax.axis_size("fsdp")
    t = lax.axis_index("tensor").reshape(1)
    left_below, left_above = around(left_root, 1), around(left_root, -1)
    routed, *cuts = route(t, block_owner, gradient, right_root, owners)
    roots = [around(c, k) for c, k in zip(cuts, (1, 2, 3))]
    onward = pick(left_below, left_above, 0, 1, left_root.shape[1:], 2 * 10**11, WHOLE)
    root_below, root_far, root_above = roots
    onward, root_below, root_above = lax.optimization_barrier((onward, root_below, root_above))
    left_far = [around(onward[0], 1), around(onward[1], -1)]
    owned = exchange(routed)
    owned, left_far, root_far = lax.optimization_barrier((owned, left_far, root_far))
    below, above = around(owned, 1), around(owned, -1)
    lefts = (left_root, left_below, left_above)
    raw, square, left = own_part(t, lefts, left_far, owned, right_root)
    below, above, raw = lax.optimization_barrier((below, above, raw))
    half = owners // 2
    shape = (half,) + owned.shape[1:]
    upper, lower = pick(below, above, pl.ds(0, half), pl.ds(half, half), shape, 3 * 10**10, PARAMS)
    halves = around(upper, 1), around(lower, -1)
    grads = (owned, below, above)
    raw = near_part(raw, left, below, above, root_below, root_above)
    raw, sums = far_part(raw, square, left, halves, root_far)
    returned = exchange(scale(t, raw, [sums] + [around(sums, k) for k in (1, 2, 3)], routed.shape))
    new_left, new_right = statistics(t, grads, halves, left_stat, right_stat)
    return (new_left, new_right, collect(block_owner, returned))


def solution(mesh):
    return jax.shard_map(
        on_device,
        mesh=mesh,
        in_specs=(
            P(None, "fsdp", "tensor"),
            P("fsdp", "tensor", None),
            P("fsdp", "tensor", None),
            P("fsdp", "tensor", None),
            P("fsdp", "tensor", None),
            P(),
        ),
        out_specs=(P("fsdp", "tensor", None), P("fsdp", "tensor", None), P(None, "fsdp", "tensor")),
        check_vma=False,
    )
```

```python
import functools

import jax
import jax.numpy as jnp
from jax import lax
from jax.experimental import pallas as pl
from jax.experimental.pallas import tpu as pltpu
from jax.sharding import PartitionSpec as P

DECAY = 0.99
EPSILON = 1e-06
BF16 = jnp.bfloat16
F32 = jnp.float32
VMEM_SPEC = pl.BlockSpec(memory_space=pltpu.VMEM)
SMEM_SPEC = pl.BlockSpec(memory_space=pltpu.SMEM)
HBM_SPEC = pl.BlockSpec(memory_space=pltpu.HBM)
PARAMS = pltpu.CompilerParams(vmem_limit_bytes=20 * 1024 * 1024)
WHOLE = pltpu.CompilerParams(vmem_limit_bytes=63 * 1024 * 1024)


def dot(a, b, ca=1, cb=0):
    return lax.dot_general(a, b, (((ca,), (cb,)), ((), ())), preferred_element_type=F32)


def cost(flops, nbytes):
    return pl.CostEstimate(flops=flops, bytes_accessed=nbytes, transcendentals=0)


def clear_counts(count_ref, owners):
    def clear(i, _):
        count_ref[i] = 0
        return 0

    lax.fori_loop(0, owners, clear, 0, unroll=8)


def route_kernel(
    t_ref, owner_hbm, grad_hbm, left_hbm, right_hbm, out_hbm, c1, c2, c3,
    grad, out, left, right, owner_ref, count_ref, sems,
):
    bring = [
        pltpu.make_async_copy(owner_hbm, owner_ref, sems.at[0]),
        pltpu.make_async_copy(grad_hbm, grad, sems.at[1]),
        pltpu.make_async_copy(left_hbm, left, sems.at[2]),
        pltpu.make_async_copy(right_hbm, right, sems.at[3]),
    ]
    for c in bring:
        c.start()
    out[...] = jnp.zeros_like(out)
    clear_counts(count_ref, out.shape[0])
    for c in bring:
        c.wait()
    rows = left.shape[1]
    half = rows // 2
    width = right.shape[2] // 4
    sends = []
    for k, cut in ((1, c1), (2, c2), (3, c3)):
        d = lax.rem(t_ref[0] + k, 4)
        slot = d // 2
        pieces = [(left.at[slot], cut.at[pl.ds(0, rows)])]
        for i, group in enumerate((d, 3 - d)):
            cols = pl.ds(pl.multiple_of(group * width, width), width)
            for j in range(2):
                source = right.at[slot, pl.ds(j * half, half), cols]
                place = cut.at[pl.ds(rows, half), pl.ds((2 * i + j) * width, width)]
                pieces.append((source, place))
        for i, (source, place) in enumerate(pieces):
            sends.append(pltpu.make_async_copy(source, place, sems.at[4 + 5 * (k - 1) + i]))
    for c in sends:
        c.start()

    def body(b, _):
        o = owner_ref[b]
        c = count_ref[o]
        count_ref[o] = c + 1
        out[o, c] = grad[b]
        return 0

    lax.fori_loop(0, grad.shape[0], body, 0, unroll=8)
    sends.append(pltpu.make_async_copy(out, out_hbm, sems.at[19]))
    sends[-1].start()
    for c in sends:
        c.wait()


def route(t, block_owner, gradient, left_root, right_root, owners):
    blocks, rows, cols = gradient.shape
    shape = (owners, 2, rows, cols)
    _, held, full = left_root.shape
    cut = jax.ShapeDtypeStruct((held + held // 2, full), BF16)
    return pl.pallas_call(
        route_kernel,
        out_shape=(jax.ShapeDtypeStruct(shape, gradient.dtype), cut, cut, cut),
        in_specs=[SMEM_SPEC] + [HBM_SPEC] * 4,
        out_specs=(HBM_SPEC,) * 4,
        scratch_shapes=[
            pltpu.VMEM(gradient.shape, BF16),
            pltpu.VMEM(shape, BF16),
            pltpu.VMEM(left_root.shape, BF16),
            pltpu.VMEM(right_root.shape, BF16),
            pltpu.SMEM((blocks,), jnp.int32),
            pltpu.SMEM((owners,), jnp.int32),
            pltpu.SemaphoreType.DMA((20,)),
        ],
        compiler_params=WHOLE,
        cost_estimate=cost(0, 3 * gradient.size),
        name="route",
    )(t, block_owner, gradient, left_root, right_root)


def collect_kernel(owner_hbm, slots_hbm, out_hbm, slots, out, owner_ref, count_ref, sems):
    bring = [
        pltpu.make_async_copy(owner_hbm, owner_ref, sems.at[0]),
        pltpu.make_async_copy(slots_hbm, slots, sems.at[1]),
    ]
    for c in bring:
        c.start()
    clear_counts(count_ref, slots.shape[0])
    for c in bring:
        c.wait()

    def body(b, _):
        o = owner_ref[b]
        c = count_ref[o]
        count_ref[o] = c + 1
        out[b] = slots[o, c]
        return 0

    lax.fori_loop(0, out.shape[0], body, 0, unroll=8)
    send = pltpu.make_async_copy(out, out_hbm, sems.at[2])
    send.start()
    send.wait()


def collect(block_owner, slots):
    blocks = block_owner.shape[0]
    shape = (blocks,) + slots.shape[2:]
    return pl.pallas_call(
        collect_kernel,
        out_shape=jax.ShapeDtypeStruct(shape, slots.dtype),
        in_specs=[HBM_SPEC] * 2,
        out_specs=HBM_SPEC,
        scratch_shapes=[
            pltpu.VMEM(slots.shape, slots.dtype),
            pltpu.VMEM(shape, slots.dtype),
            pltpu.SMEM((blocks,), jnp.int32),
            pltpu.SMEM((slots.shape[0],), jnp.int32),
            pltpu.SemaphoreType.DMA((3,)),
        ],
        compiler_params=PARAMS,
        cost_estimate=cost(0, 3 * slots.size),
        name="collect",
    )(block_owner, slots)


def select_kernel(t_ref, both_hbm, s1, s2, s3, both, sems):
    bring = pltpu.make_async_copy(both_hbm, both, sems.at[0])
    bring.start()
    bring.wait()
    sends = []
    for k, out in ((1, s1), (2, s2), (3, s3)):
        slot = lax.rem(t_ref[0] + k, 4) // 2
        sends.append(pltpu.make_async_copy(both.at[:, slot], out, sems.at[k]))
        sends[-1].start()
    for c in sends:
        c.wait()


def select(t, both):
    owners, _, height, width = both.shape
    out = jax.ShapeDtypeStruct((owners, height, width), BF16)
    return pl.pallas_call(
        select_kernel,
        out_shape=(out,) * 3,
        in_specs=[SMEM_SPEC, HBM_SPEC],
        out_specs=(HBM_SPEC,) * 3,
        scratch_shapes=[pltpu.VMEM(both.shape, BF16), pltpu.SemaphoreType.DMA((4,))],
        compiler_params=PARAMS,
        cost_estimate=cost(0, 6 * both.size),
        name="select",
    )(t, both)


def bring_right(cut, to, sems):
    _, rows, width = to.shape
    half = rows // 2
    return [
        pltpu.make_async_copy(
            cut.at[pl.ds(rows, half), pl.ds((2 * i + j) * width, width)],
            to.at[i, pl.ds(j * half, half)],
            sems.at[2 * i + j],
        )
        for i in range(2)
        for j in range(2)
    ]


def hold_kernel(a, b, out_ref):
    out_ref[...] = jnp.zeros_like(out_ref)


def hold(first, second):
    return pl.pallas_call(
        hold_kernel,
        out_shape=jax.ShapeDtypeStruct((8, 128), F32),
        in_specs=[HBM_SPEC] * 2,
        out_specs=VMEM_SPEC,
        compiler_params=WHOLE,
        cost_estimate=cost(2 * 10**11, 8 * 128),
        name="hold",
    )(first, second)


def own_kernel(
    t_ref, token, left_hbm, right_hbm, c1, c3, c2, both_hbm, raw_ref, square_ref, left, both, roots, sems
):
    t = t_ref[0]
    slot = t // 2
    rows = left_hbm.shape[1]
    full = left.shape[0]
    width = roots.shape[2]
    bring = [
        pltpu.make_async_copy(both_hbm, both, sems.at[0]),
        pltpu.make_async_copy(left_hbm.at[slot], left.at[pl.ds(0, rows)], sems.at[1]),
    ]
    for i, c in enumerate((c1, c3, c2)):
        to = left.at[pl.ds((i + 1) * rows, rows)]
        bring.append(pltpu.make_async_copy(c.at[pl.ds(0, rows)], to, sems.at[2 + i]))
    for i, group in enumerate((t, 3 - t)):
        cols = pl.ds(pl.multiple_of(group * width, width), width)
        bring.append(pltpu.make_async_copy(right_hbm.at[slot, :, cols], roots.at[i], sems.at[5 + i]))
    for c in bring:
        c.start()
    for c in bring:
        c.wait()
    part = dot(left[...], both[:, slot].reshape(full, width)).astype(BF16)
    for i in range(2):
        raw_ref[i] = dot(part, roots[i])
    for i in range(2):
        wide = both[:, i].reshape(full, width).astype(F32)
        square_ref[i] = jnp.broadcast_to(jnp.sum(wide * wide, keepdims=True), square_ref.shape[1:])


def own_part(t, token, left_root, right_root, cuts, owned):
    owners, slots, height, width = owned.shape
    full = owners * height
    return pl.pallas_call(
        own_kernel,
        out_shape=(
            jax.ShapeDtypeStruct((2, full, width), F32),
            jax.ShapeDtypeStruct((slots, 8, 128), F32),
            jax.ShapeDtypeStruct((full, full), BF16),
        ),
        in_specs=[SMEM_SPEC, VMEM_SPEC] + [HBM_SPEC] * 6,
        out_specs=(VMEM_SPEC,) * 3,
        scratch_shapes=[
            pltpu.VMEM(owned.shape, BF16),
            pltpu.VMEM((2, width, width), BF16),
            pltpu.SemaphoreType.DMA((7,)),
        ],
        compiler_params=PARAMS,
        cost_estimate=cost(4 * full * full * width, 12 * full * full),
        name="own_part",
    )(t, token, left_root, right_root, *cuts, owned)


def near_kernel(own, left, g1, g3, c1, c3, raw_ref, grads, roots, sems):
    full = left.shape[0]
    width = roots.shape[3]
    groups = []
    for i, (g, c) in enumerate(((g1, c1), (g3, c3))):
        bring = [pltpu.make_async_copy(g, grads.at[i], sems.at[i, 4])]
        groups.append(bring + bring_right(c, roots.at[i], sems.at[i]))
    for bring in groups:
        for c in bring:
            c.start()
    raw = [own[0], own[1]]
    for i, bring in enumerate(groups):
        for c in bring:
            c.wait()
        part = dot(left[...], grads[i].reshape(full, width)).astype(BF16)
        for j in range(2):
            raw[j] = raw[j] + dot(part, roots[i, j])
    for j in range(2):
        raw_ref[j] = raw[j]


def near_part(own, left, below, above, cut_below, cut_above):
    owners, height, width = below.shape
    full = left.shape[0]
    return pl.pallas_call(
        near_kernel,
        out_shape=jax.ShapeDtypeStruct(own.shape, F32),
        in_specs=[VMEM_SPEC] * 2 + [HBM_SPEC] * 4,
        out_specs=VMEM_SPEC,
        scratch_shapes=[
            pltpu.VMEM((2, owners, height, width), BF16),
            pltpu.VMEM((2, 2, width, width), BF16),
            pltpu.SemaphoreType.DMA((2, 5)),
        ],
        compiler_params=PARAMS,
        cost_estimate=cost(6 * full * full * width, 10 * full * full),
        name="near_part",
    )(own, left, below, above, cut_below, cut_above)


def far_kernel(
    t_ref, near, square, left, g2, c2, mine_ref, other_ref, sums_ref, roots, sems
):
    bring = bring_right(c2, roots, sems)
    for c in bring:
        c.start()
    full = left.shape[0]
    width = roots.shape[2]
    part = dot(left[...], g2[...].reshape(full, width)).astype(BF16)
    for c in bring:
        c.wait()
    mine = near[0] + dot(part, roots[0])
    other = near[1] + dot(part, roots[1])
    mine_ref[...] = mine
    other_ref[...] = other.astype(BF16)
    total = jnp.sum(mine * mine, keepdims=True) + jnp.sum(other * other, keepdims=True)
    row = lax.broadcasted_iota(jnp.int32, sums_ref.shape, 0)
    sums = jnp.where(row == t_ref[0] // 2, total, jnp.zeros(sums_ref.shape, F32))
    for slot in range(2):
        sums = jnp.where(row == 2 + slot, square[slot], sums)
    sums_ref[...] = sums


def far_part(t, near, square, left, far, cut_far):
    _, full, width = near.shape
    return pl.pallas_call(
        far_kernel,
        out_shape=(
            jax.ShapeDtypeStruct((full, width), F32),
            jax.ShapeDtypeStruct((full, width), BF16),
            jax.ShapeDtypeStruct((8, 128), F32),
        ),
        in_specs=[SMEM_SPEC] + [VMEM_SPEC] * 4 + [HBM_SPEC],
        out_specs=(VMEM_SPEC,) * 3,
        scratch_shapes=[pltpu.VMEM((2, width, width), BF16), pltpu.SemaphoreType.DMA((4,))],
        compiler_params=PARAMS,
        cost_estimate=cost(4 * full * full * width, 8 * full * full),
        name="far_part",
    )(t, near, square, left, far, cut_far)


def scale_kernel(t_ref, mine, other, s0, s1, s2, s3, out_hbm, ready, sems):
    _, _, here, height, width = ready.shape
    rows = here * height
    t = t_ref[0]
    sums = s0[...] + s1[...] + s2[...] + s3[...]
    first, second = (
        jnp.sqrt((sums[2 + slot : 3 + slot, 0:1] + EPSILON) / (sums[slot : slot + 1, 0:1] + EPSILON))
        for slot in range(2)
    )
    copies = []
    for j, (raw, member) in enumerate(((mine, t), (other, 3 - t))):
        slot = member // 2
        graft = jnp.where(slot == 0, first, second)
        for i, k in enumerate((0, 1, 3, 2)):
            scaled = raw[i * rows : (i + 1) * rows, :].astype(F32) * graft
            ready[j, i] = scaled.astype(BF16).reshape(here, height, width)
            s = lax.rem(member + 4 - k, 4)
            to = out_hbm.at[pl.ds(s * here, here), slot]
            copies.append(pltpu.make_async_copy(ready.at[j, i], to, sems.at[j, i]))
            copies[-1].start()
    for c in copies:
        c.wait()


def scale(t, mine, other, sums, shape):
    owners, _, height, width = shape
    return pl.pallas_call(
        scale_kernel,
        out_shape=jax.ShapeDtypeStruct(shape, BF16),
        in_specs=[SMEM_SPEC] + [VMEM_SPEC] * 6,
        out_specs=HBM_SPEC,
        scratch_shapes=[
            pltpu.VMEM((2, 4, owners // 4, height, width), BF16),
            pltpu.SemaphoreType.DMA((2, 4)),
        ],
        compiler_params=PARAMS,
        cost_estimate=cost(0, 16 * owners * height * width),
        name="scale",
    )(t, mine, other, *sums)


def terms_kernel(t_ref, g0_hbm, g1, g3, g2, out_ref, own, turned, sems):
    t = t_ref[0]
    bring = pltpu.make_async_copy(g0_hbm.at[:, t // 2], own, sems.at[0])
    bring.start()
    owners, height, rows = own.shape
    full = owners * height
    here = owners // 4
    theirs = pl.ds(pl.multiple_of((3 - t) * here, here), here)

    def turn(g):
        turned[...] = g[...].reshape(full, rows).T

    pl.when(lax.rem(t, 2) == 0)(lambda: turn(g1))
    pl.when(lax.rem(t, 2) == 1)(lambda: turn(g3))
    bring.wait()
    term = None
    for k, g in ((0, own), (1, g1), (3, g3), (2, g2)):
        whole = g[...].reshape(full, rows)
        part = dot(g[theirs].reshape(rows, rows), whole, 1, 1)
        term = part if term is None else term + part
        s = lax.rem(t + 4 - k, 4)
        cols = pl.ds(pl.multiple_of(s * rows, rows), rows)
        out_ref[1, :, cols] = dot(turned[...], whole).astype(BF16)
    out_ref[0] = term.astype(BF16)


def terms_across(t, owned, others):
    owners, _, height, rows = owned.shape
    full = owners * height
    return pl.pallas_call(
        terms_kernel,
        out_shape=jax.ShapeDtypeStruct((2, rows, full), BF16),
        in_specs=[SMEM_SPEC, HBM_SPEC] + [VMEM_SPEC] * 3,
        out_specs=VMEM_SPEC,
        scratch_shapes=[
            pltpu.VMEM((owners, height, rows), BF16),
            pltpu.VMEM((rows, full), BF16),
            pltpu.SemaphoreType.DMA((1,)),
        ],
        compiler_params=PARAMS,
        cost_estimate=cost(4 * rows * full * full, 6 * rows * full),
        name="terms_across",
    )(t, owned, *others)


def stats_kernel(t_ref, g0_hbm, g1, g3, g2, left_ref, right_ref, new_left_ref, new_right_ref, own, sems):
    t = t_ref[0]
    rows, full = left_ref.shape
    here = own.shape[0] // 4
    mine = pl.ds(pl.multiple_of(t * here, here), here)
    bring = pltpu.make_async_copy(g0_hbm.at[:, t // 2], own, sems.at[0])
    bring.start()
    bring.wait()
    turned = own[...].reshape(full, rows).T
    term = None
    for k, g in ((0, own), (1, g1), (3, g3), (2, g2)):
        whole = g[...].reshape(full, rows)
        part = dot(g[mine].reshape(rows, rows), whole, 1, 1)
        term = part if term is None else term + part
        s = lax.rem(t + 4 - k, 4)
        cols = pl.ds(pl.multiple_of(s * rows, rows), rows)
        new_right_ref[:, cols] = DECAY * right_ref[:, cols] + (1.0 - DECAY) * dot(turned, whole)
    new_left_ref[...] = DECAY * left_ref[...] + (1.0 - DECAY) * term


def statistics(t, owned, others, left_stat, right_stat):
    _, rows, full = left_stat.shape
    owners, _, height, width = owned.shape
    slot_spec = pl.BlockSpec((None, rows, full), lambda i, t_ref: (t_ref[0] // 2, 0, 0))
    shape = jax.ShapeDtypeStruct(left_stat.shape, F32)
    return pl.pallas_call(
        stats_kernel,
        out_shape=(shape, shape),
        grid_spec=pltpu.PrefetchScalarGridSpec(
            num_scalar_prefetch=1,
            grid=(1,),
            in_specs=[HBM_SPEC] + [VMEM_SPEC] * 3 + [slot_spec] * 2,
            out_specs=(slot_spec, slot_spec),
            scratch_shapes=[pltpu.VMEM((owners, height, width), BF16), pltpu.SemaphoreType.DMA((1,))],
        ),
        compiler_params=pltpu.CompilerParams(vmem_limit_bytes=32 * 1024 * 1024),
        cost_estimate=cost(4 * rows * full * full, 12 * rows * full),
        name="statistics",
    )(t, owned, *others, left_stat, right_stat)


def blend_kernel(t_ref, terms, left_ref, right_ref, _, __, new_left_ref, new_right_ref):
    new_left_ref[...] = DECAY * left_ref[...] + (1.0 - DECAY) * terms[0].astype(F32)
    new_right_ref[...] = DECAY * right_ref[...] + (1.0 - DECAY) * terms[1].astype(F32)


def blend(t, terms, left_stat, right_stat, done):
    _, rows, full = left_stat.shape
    slot_spec = pl.BlockSpec((None, rows, full), lambda i, t_ref: (1 - t_ref[0] // 2, 0, 0))
    shape = jax.ShapeDtypeStruct(left_stat.shape, F32)
    return pl.pallas_call(
        blend_kernel,
        out_shape=(shape, shape),
        grid_spec=pltpu.PrefetchScalarGridSpec(
            num_scalar_prefetch=1,
            grid=(1,),
            in_specs=[VMEM_SPEC] + [slot_spec] * 2 + [HBM_SPEC] * 2,
            out_specs=(slot_spec, slot_spec),
        ),
        input_output_aliases={4: 0, 5: 1},
        compiler_params=pltpu.CompilerParams(vmem_limit_bytes=32 * 1024 * 1024),
        cost_estimate=cost(4 * rows * full, 18 * rows * full),
        name="blend",
    )(t, terms, left_stat, right_stat, *done)


def around(x, k):
    n = lax.axis_size("tensor")
    return lax.ppermute(x, "tensor", [(i, (i + k) % n) for i in range(n)])


def across(x):
    n = lax.axis_size("tensor")
    return lax.ppermute(x, "tensor", [(i, n - 1 - i) for i in range(n)])


def exchange(x):
    return lax.all_to_all(x, "fsdp", split_axis=0, concat_axis=0, tiled=True)


def on_device(gradient, left_stat, right_stat, left_root, right_root, block_owner):
    owners = lax.axis_size("fsdp")
    t = lax.axis_index("tensor").reshape(1)
    routed, *cuts = route(t, block_owner, gradient, left_root, right_root, owners)
    cut_below, cut_far, cut_above = (around(c, k) for c, k in zip(cuts, (1, 2, 3)))
    owned = exchange(routed)
    owned, token = lax.optimization_barrier((owned, hold(cut_below, cut_above)))
    below, far, above = (around(x, k) for x, k in zip(select(t, owned), (1, 2, 3)))
    cuts = (cut_below, cut_above, cut_far)
    raw, square, left = own_part(t, token, left_root, right_root, cuts, owned)
    raw = near_part(raw, left, below, above, cut_below, cut_above)
    mine, other, sums = far_part(t, raw, square, left, far, cut_far)
    other = across(other)
    everyone = [sums] + [around(sums, k) for k in (1, 2, 3)]
    others = (below, above, far)
    terms = terms_across(t, owned, others)
    everyone, terms = lax.optimization_barrier((everyone, terms))
    terms = across(terms)
    returned = exchange(scale(t, mine, other, everyone, routed.shape))
    done = statistics(t, owned, others, left_stat, right_stat)
    new_left, new_right = blend(t, terms, left_stat, right_stat, done)
    return (new_left, new_right, collect(block_owner, returned))


def solution(mesh):
    return jax.shard_map(
        on_device,
        mesh=mesh,
        in_specs=(
            P(None, "fsdp", "tensor"),
            P("fsdp", "tensor", None),
            P("fsdp", "tensor", None),
            P("fsdp", "tensor", None),
            P("fsdp", "tensor", None),
            P(),
        ),
        out_specs=(P("fsdp", "tensor", None), P("fsdp", "tensor", None), P(None, "fsdp", "tensor")),
        check_vma=False,
    )
```

```python
import functools

import jax
import jax.numpy as jnp
from jax import lax
from jax.experimental import pallas as pl
from jax.experimental.pallas import tpu as pltpu
from jax.sharding import PartitionSpec as P

DECAY = 0.99
EPSILON = 1e-06
BF16 = jnp.bfloat16
F32 = jnp.float32
VMEM_SPEC = pl.BlockSpec(memory_space=pltpu.VMEM)
SMEM_SPEC = pl.BlockSpec(memory_space=pltpu.SMEM)
HBM_SPEC = pl.BlockSpec(memory_space=pltpu.HBM)
PARAMS = pltpu.CompilerParams(vmem_limit_bytes=20 * 1024 * 1024)
WHOLE = pltpu.CompilerParams(vmem_limit_bytes=63 * 1024 * 1024)


def dot(a, b, ca=1, cb=0):
    return lax.dot_general(a, b, (((ca,), (cb,)), ((), ())), preferred_element_type=F32)


def cost(flops, nbytes):
    return pl.CostEstimate(flops=flops, bytes_accessed=nbytes, transcendentals=0)


def clear_counts(count_ref, owners):
    def clear(i, _):
        count_ref[i] = 0
        return 0

    lax.fori_loop(0, owners, clear, 0, unroll=8)


def column_groups(member, width):
    half = width // 2
    after, before = lax.rem(member + 1, 4), lax.rem(member + 3, 4)
    return (member * width, width, 0), (after * width, half, width), (before * width + half, half, width + half)


def route_kernel(
    t_ref, owner_hbm, grad_hbm, left_hbm, right_hbm, out_hbm, c1, c2, c3,
    grad, out, left, right, owner_ref, count_ref, sems,
):
    bring = [
        pltpu.make_async_copy(owner_hbm, owner_ref, sems.at[0]),
        pltpu.make_async_copy(grad_hbm, grad, sems.at[1]),
        pltpu.make_async_copy(left_hbm, left, sems.at[2]),
        pltpu.make_async_copy(right_hbm, right, sems.at[3]),
    ]
    for c in bring:
        c.start()
    out[...] = jnp.zeros_like(out)
    clear_counts(count_ref, out.shape[0])
    for c in bring:
        c.wait()
    rows = left.shape[1]
    half = rows // 2
    width = right.shape[2] // 4
    sends = []
    for k, cut in ((1, c1), (2, c2), (3, c3)):
        d = lax.rem(t_ref[0] + k, 4)
        slot = lax.rem(d, 2)
        pieces = [(left.at[slot], cut.at[pl.ds(0, rows)])]
        for j in range(2):
            for start, size, at in column_groups(d, width):
                source = right.at[slot, pl.ds(j * half, half), pl.ds(pl.multiple_of(start, 128), size)]
                at = at + j * width if size == width else at + (j + 1) * width
                pieces.append((source, cut.at[pl.ds(rows, half), pl.ds(at, size)]))
        for i, (source, place) in enumerate(pieces):
            sends.append(pltpu.make_async_copy(source, place, sems.at[4 + 7 * (k - 1) + i]))
    for c in sends:
        c.start()

    def body(b, _):
        o = owner_ref[b]
        c = count_ref[o]
        count_ref[o] = c + 1
        out[o, c] = grad[b]
        return 0

    lax.fori_loop(0, grad.shape[0], body, 0, unroll=8)
    sends.append(pltpu.make_async_copy(out, out_hbm, sems.at[25]))
    sends[-1].start()
    for c in sends:
        c.wait()


def route(t, block_owner, gradient, left_root, right_root, owners):
    blocks, rows, cols = gradient.shape
    shape = (owners, 2, rows, cols)
    _, held, full = left_root.shape
    cut = jax.ShapeDtypeStruct((held + held // 2, full), BF16)
    return pl.pallas_call(
        route_kernel,
        out_shape=(jax.ShapeDtypeStruct(shape, gradient.dtype), cut, cut, cut),
        in_specs=[SMEM_SPEC] + [HBM_SPEC] * 4,
        out_specs=(HBM_SPEC,) * 4,
        scratch_shapes=[
            pltpu.VMEM(gradient.shape, BF16),
            pltpu.VMEM(shape, BF16),
            pltpu.VMEM(left_root.shape, BF16),
            pltpu.VMEM(right_root.shape, BF16),
            pltpu.SMEM((blocks,), jnp.int32),
            pltpu.SMEM((owners,), jnp.int32),
            pltpu.SemaphoreType.DMA((26,)),
        ],
        compiler_params=WHOLE,
        cost_estimate=cost(0, 3 * gradient.size),
        name="route",
    )(t, block_owner, gradient, left_root, right_root)


def collect_kernel(owner_hbm, slots_hbm, out_hbm, slots, out, owner_ref, count_ref, sems):
    bring = [
        pltpu.make_async_copy(owner_hbm, owner_ref, sems.at[0]),
        pltpu.make_async_copy(slots_hbm, slots, sems.at[1]),
    ]
    for c in bring:
        c.start()
    clear_counts(count_ref, slots.shape[0])
    for c in bring:
        c.wait()

    def body(b, _):
        o = owner_ref[b]
        c = count_ref[o]
        count_ref[o] = c + 1
        out[b] = slots[o, c]
        return 0

    lax.fori_loop(0, out.shape[0], body, 0, unroll=8)
    send = pltpu.make_async_copy(out, out_hbm, sems.at[2])
    send.start()
    send.wait()


def collect(block_owner, slots):
    blocks = block_owner.shape[0]
    shape = (blocks,) + slots.shape[2:]
    return pl.pallas_call(
        collect_kernel,
        out_shape=jax.ShapeDtypeStruct(shape, slots.dtype),
        in_specs=[HBM_SPEC] * 2,
        out_specs=HBM_SPEC,
        scratch_shapes=[
            pltpu.VMEM(slots.shape, slots.dtype),
            pltpu.VMEM(shape, slots.dtype),
            pltpu.SMEM((blocks,), jnp.int32),
            pltpu.SMEM((slots.shape[0],), jnp.int32),
            pltpu.SemaphoreType.DMA((3,)),
        ],
        compiler_params=PARAMS,
        cost_estimate=cost(0, 3 * slots.size),
        name="collect",
    )(block_owner, slots)


def select_kernel(t_ref, both_hbm, other_hbm, same_hbm, both, sems):
    bring = pltpu.make_async_copy(both_hbm, both, sems.at[0])
    bring.start()
    bring.wait()
    slot = lax.rem(t_ref[0], 2)
    sends = [
        pltpu.make_async_copy(both.at[:, 1 - slot], other_hbm, sems.at[1]),
        pltpu.make_async_copy(both.at[:, slot], same_hbm, sems.at[2]),
    ]
    for c in sends:
        c.start()
    for c in sends:
        c.wait()


def select(t, both):
    owners, _, height, width = both.shape
    out = jax.ShapeDtypeStruct((owners, height, width), BF16)
    return pl.pallas_call(
        select_kernel,
        out_shape=(out,) * 2,
        in_specs=[SMEM_SPEC, HBM_SPEC],
        out_specs=(HBM_SPEC,) * 2,
        scratch_shapes=[pltpu.VMEM(both.shape, BF16), pltpu.SemaphoreType.DMA((3,))],
        compiler_params=PARAMS,
        cost_estimate=cost(0, 4 * both.size),
        name="select",
    )(t, both)


def bring_right(cut, to, sems):
    _, rows, width = to.shape
    half = rows // 2
    return [
        pltpu.make_async_copy(
            cut.at[pl.ds(rows, half), pl.ds((2 * i + j) * width, width)],
            to.at[i, pl.ds(j * half, half)],
            sems.at[2 * i + j],
        )
        for i in range(2)
        for j in range(2)
    ]


def hold_kernel(a, b, out_ref):
    out_ref[...] = jnp.zeros_like(out_ref)


def hold(first, second):
    return pl.pallas_call(
        hold_kernel,
        out_shape=jax.ShapeDtypeStruct((8, 128), F32),
        in_specs=[HBM_SPEC] * 2,
        out_specs=VMEM_SPEC,
        compiler_params=WHOLE,
        cost_estimate=cost(2 * 10**11, 8 * 128),
        name="hold",
    )(first, second)


def own_kernel(
    t_ref, token, left_hbm, right_hbm, c1, c3, c2, both_hbm, raw_ref, square_ref, left, both, roots, sems
):
    t = t_ref[0]
    slot = lax.rem(t, 2)
    rows = left_hbm.shape[1]
    full = left.shape[0]
    width = roots.shape[2]
    bring = [
        pltpu.make_async_copy(both_hbm, both, sems.at[0]),
        pltpu.make_async_copy(left_hbm.at[slot], left.at[pl.ds(0, rows)], sems.at[1]),
    ]
    for i, c in enumerate((c1, c3, c2)):
        to = left.at[pl.ds((i + 1) * rows, rows)]
        bring.append(pltpu.make_async_copy(c.at[pl.ds(0, rows)], to, sems.at[2 + i]))
    for i, (start, size, at) in enumerate(column_groups(t, width)):
        source = right_hbm.at[slot, :, pl.ds(pl.multiple_of(start, 128), size)]
        to = roots.at[at // width, :, pl.ds(at % width, size)]
        bring.append(pltpu.make_async_copy(source, to, sems.at[5 + i]))
    for c in bring:
        c.start()
    for c in bring:
        c.wait()
    part = dot(left[...], both[:, slot].reshape(full, width)).astype(BF16)
    for i in range(2):
        raw_ref[i] = dot(part, roots[i])
    for i in range(2):
        wide = both[:, i].reshape(full, width).astype(F32)
        square_ref[i] = jnp.broadcast_to(jnp.sum(wide * wide, keepdims=True), square_ref.shape[1:])


def own_part(t, token, left_root, right_root, cuts, owned):
    owners, slots, height, width = owned.shape
    full = owners * height
    return pl.pallas_call(
        own_kernel,
        out_shape=(
            jax.ShapeDtypeStruct((2, full, width), F32),
            jax.ShapeDtypeStruct((slots, 8, 128), F32),
            jax.ShapeDtypeStruct((full, full), BF16),
        ),
        in_specs=[SMEM_SPEC, VMEM_SPEC] + [HBM_SPEC] * 6,
        out_specs=(VMEM_SPEC,) * 3,
        scratch_shapes=[
            pltpu.VMEM(owned.shape, BF16),
            pltpu.VMEM((2, width, width), BF16),
            pltpu.SemaphoreType.DMA((8,)),
        ],
        compiler_params=PARAMS,
        cost_estimate=cost(4 * full * full * width, 12 * full * full),
        name="own_part",
    )(t, token, left_root, right_root, *cuts, owned)


def near_kernel(own, left, g1, g3, c1, c3, raw_ref, grads, roots, sems):
    full = left.shape[0]
    width = roots.shape[3]
    groups = []
    for i, (g, c) in enumerate(((g1, c1), (g3, c3))):
        bring = [pltpu.make_async_copy(g, grads.at[i], sems.at[i, 4])]
        groups.append(bring + bring_right(c, roots.at[i], sems.at[i]))
    for bring in groups:
        for c in bring:
            c.start()
    raw = [own[0], own[1]]
    for i, bring in enumerate(groups):
        for c in bring:
            c.wait()
        part = dot(left[...], grads[i].reshape(full, width)).astype(BF16)
        for j in range(2):
            raw[j] = raw[j] + dot(part, roots[i, j])
    for j in range(2):
        raw_ref[j] = raw[j]


def near_part(own, left, below, above, cut_below, cut_above):
    owners, height, width = below.shape
    full = left.shape[0]
    return pl.pallas_call(
        near_kernel,
        out_shape=jax.ShapeDtypeStruct(own.shape, F32),
        in_specs=[VMEM_SPEC] * 2 + [HBM_SPEC] * 4,
        out_specs=VMEM_SPEC,
        scratch_shapes=[
            pltpu.VMEM((2, owners, height, width), BF16),
            pltpu.VMEM((2, 2, width, width), BF16),
            pltpu.SemaphoreType.DMA((2, 5)),
        ],
        compiler_params=PARAMS,
        cost_estimate=cost(6 * full * full * width, 10 * full * full),
        name="near_part",
    )(own, left, below, above, cut_below, cut_above)


def far_kernel(
    t_ref, near, square, left, g2, c2, mine_ref, after_ref, before_ref, sums_ref, roots, sems
):
    bring = bring_right(c2, roots, sems)
    for c in bring:
        c.start()
    full = left.shape[0]
    width = roots.shape[2]
    part = dot(left[...], g2[...].reshape(full, width)).astype(BF16)
    for c in bring:
        c.wait()
    mine = near[0] + dot(part, roots[0])
    other = near[1] + dot(part, roots[1])
    mine_ref[...] = mine
    after_ref[...] = other[:, : width // 2].astype(BF16)
    before_ref[...] = other[:, width // 2 :].astype(BF16)
    total = jnp.sum(mine * mine, keepdims=True) + jnp.sum(other * other, keepdims=True)
    row = lax.broadcasted_iota(jnp.int32, sums_ref.shape, 0)
    sums = jnp.where(row == lax.rem(t_ref[0], 2), total, jnp.zeros(sums_ref.shape, F32))
    for slot in range(2):
        sums = jnp.where(row == 2 + slot, square[slot], sums)
    sums_ref[...] = sums


def far_part(t, near, square, left, far, cut_far):
    _, full, width = near.shape
    half = jax.ShapeDtypeStruct((full, width // 2), BF16)
    return pl.pallas_call(
        far_kernel,
        out_shape=(
            jax.ShapeDtypeStruct((full, width), F32),
            half,
            half,
            jax.ShapeDtypeStruct((8, 128), F32),
        ),
        in_specs=[SMEM_SPEC] + [VMEM_SPEC] * 4 + [HBM_SPEC],
        out_specs=(VMEM_SPEC,) * 4,
        scratch_shapes=[pltpu.VMEM((2, width, width), BF16), pltpu.SemaphoreType.DMA((4,))],
        compiler_params=PARAMS,
        cost_estimate=cost(4 * full * full * width, 8 * full * full),
        name="far_part",
    )(t, near, square, left, far, cut_far)


def scale_kernel(t_ref, mine, first, second, s0, s1, s2, s3, out_hbm, ready, halves, sems):
    _, here, height, width = ready.shape
    rows = here * height
    t = t_ref[0]
    sums = s0[...] + s1[...] + s2[...] + s3[...]
    grafts = [
        jnp.sqrt((sums[2 + slot : 3 + slot, 0:1] + EPSILON) / (sums[slot : slot + 1, 0:1] + EPSILON))
        for slot in range(2)
    ]
    even = lax.rem(t, 2) == 0
    own_graft = jnp.where(even, grafts[0], grafts[1])
    other_graft = jnp.where(even, grafts[1], grafts[0])
    slot = lax.rem(t, 2)
    half = width // 2
    parts = (
        (mine, t, own_graft, slot, ready, pl.ds(0, width)),
        (first, t + 3, other_graft, 1 - slot, halves.at[0], pl.ds(0, half)),
        (second, t + 1, other_graft, 1 - slot, halves.at[1], pl.ds(half, half)),
    )
    copies = []
    for j, (raw, member, graft, slot, held, cols) in enumerate(parts):
        for i, k in enumerate((0, 1, 3, 2)):
            scaled = raw[i * rows : (i + 1) * rows, :].astype(F32) * graft
            held[i] = scaled.astype(BF16).reshape(here, height, held.shape[3])
            s = lax.rem(member + 4 - k, 4)
            to = out_hbm.at[pl.ds(s * here, here), slot, :, cols]
            copies.append(pltpu.make_async_copy(held.at[i], to, sems.at[j, i]))
            copies[-1].start()
    for c in copies:
        c.wait()


def scale(t, mine, first, second, sums, shape):
    owners, _, height, width = shape
    here = owners // 4
    return pl.pallas_call(
        scale_kernel,
        out_shape=jax.ShapeDtypeStruct(shape, BF16),
        in_specs=[SMEM_SPEC] + [VMEM_SPEC] * 7,
        out_specs=HBM_SPEC,
        scratch_shapes=[
            pltpu.VMEM((4, here, height, width), BF16),
            pltpu.VMEM((2, 4, here, height, width // 2), BF16),
            pltpu.SemaphoreType.DMA((3, 4)),
        ],
        compiler_params=PARAMS,
        cost_estimate=cost(0, 16 * owners * height * width),
        name="scale",
    )(t, mine, first, second, *sums)


def terms_kernel(t_ref, g0_hbm, g1, g3, g2, left_ref, right_ref, own, sems):
    t = t_ref[0]
    bring = pltpu.make_async_copy(g0_hbm.at[:, lax.rem(t, 2)], own, sems.at[0])
    bring.start()
    owners, height, rows = own.shape
    full = owners * height
    here = owners // 4
    after = pl.ds(pl.multiple_of(lax.rem(t + 1, 4) * here, here), here)
    turned = g1[...].reshape(full, rows).T
    bring.wait()
    term = None
    for k, g in ((0, own), (1, g1), (3, g3), (2, g2)):
        whole = g[...].reshape(full, rows)
        part = dot(g[after].reshape(rows, rows), whole, 1, 1)
        term = part if term is None else term + part
        s = lax.rem(t + 4 - k, 4)
        cols = pl.ds(pl.multiple_of(s * rows, rows), rows)
        right_ref[:, cols] = dot(turned, whole).astype(BF16)
    left_ref[...] = term.astype(BF16)


def neighbour_terms(t, owned, others):
    owners, _, height, rows = owned.shape
    out = jax.ShapeDtypeStruct((rows, owners * height), BF16)
    return pl.pallas_call(
        terms_kernel,
        out_shape=(out, out),
        in_specs=[SMEM_SPEC, HBM_SPEC] + [VMEM_SPEC] * 3,
        out_specs=(VMEM_SPEC, VMEM_SPEC),
        scratch_shapes=[pltpu.VMEM((owners, height, rows), BF16), pltpu.SemaphoreType.DMA((1,))],
        compiler_params=PARAMS,
        cost_estimate=cost(4 * rows * (owners * height) ** 2, 6 * rows * owners * height),
        name="neighbour_terms",
    )(t, owned, *others)


def stats_kernel(t_ref, g0_hbm, g1, g3, g2, left_ref, right_ref, new_left_ref, new_right_ref, own, sems):
    t = t_ref[0]
    rows, full = left_ref.shape
    here = own.shape[0] // 4
    mine = pl.ds(pl.multiple_of(t * here, here), here)
    bring = pltpu.make_async_copy(g0_hbm.at[:, lax.rem(t, 2)], own, sems.at[0])
    bring.start()
    bring.wait()
    turned = own[...].reshape(full, rows).T
    term = None
    for k, g in ((0, own), (1, g1), (3, g3), (2, g2)):
        whole = g[...].reshape(full, rows)
        part = dot(g[mine].reshape(rows, rows), whole, 1, 1)
        term = part if term is None else term + part
        s = lax.rem(t + 4 - k, 4)
        cols = pl.ds(pl.multiple_of(s * rows, rows), rows)
        new_right_ref[:, cols] = DECAY * right_ref[:, cols] + (1.0 - DECAY) * dot(turned, whole)
    new_left_ref[...] = DECAY * left_ref[...] + (1.0 - DECAY) * term


def statistics(t, owned, others, left_stat, right_stat):
    _, rows, full = left_stat.shape
    owners, _, height, width = owned.shape
    slot_spec = pl.BlockSpec((None, rows, full), lambda i, t_ref: (lax.rem(t_ref[0], 2), 0, 0))
    shape = jax.ShapeDtypeStruct(left_stat.shape, F32)
    return pl.pallas_call(
        stats_kernel,
        out_shape=(shape, shape),
        grid_spec=pltpu.PrefetchScalarGridSpec(
            num_scalar_prefetch=1,
            grid=(1,),
            in_specs=[HBM_SPEC] + [VMEM_SPEC] * 3 + [slot_spec] * 2,
            out_specs=(slot_spec, slot_spec),
            scratch_shapes=[pltpu.VMEM((owners, height, width), BF16), pltpu.SemaphoreType.DMA((1,))],
        ),
        compiler_params=pltpu.CompilerParams(vmem_limit_bytes=32 * 1024 * 1024),
        cost_estimate=cost(4 * rows * full * full, 12 * rows * full),
        name="statistics",
    )(t, owned, *others, left_stat, right_stat)


def blend_kernel(t_ref, left_term, right_term, left_ref, right_ref, _, __, new_left_ref, new_right_ref):
    new_left_ref[...] = DECAY * left_ref[...] + (1.0 - DECAY) * left_term[...].astype(F32)
    new_right_ref[...] = DECAY * right_ref[...] + (1.0 - DECAY) * right_term[...].astype(F32)


def blend(t, terms, left_stat, right_stat, done):
    _, rows, full = left_stat.shape
    slot_spec = pl.BlockSpec((None, rows, full), lambda i, t_ref: (1 - lax.rem(t_ref[0], 2), 0, 0))
    shape = jax.ShapeDtypeStruct(left_stat.shape, F32)
    return pl.pallas_call(
        blend_kernel,
        out_shape=(shape, shape),
        grid_spec=pltpu.PrefetchScalarGridSpec(
            num_scalar_prefetch=1,
            grid=(1,),
            in_specs=[VMEM_SPEC] * 2 + [slot_spec] * 2 + [HBM_SPEC] * 2,
            out_specs=(slot_spec, slot_spec),
        ),
        input_output_aliases={5: 0, 6: 1},
        compiler_params=pltpu.CompilerParams(vmem_limit_bytes=32 * 1024 * 1024),
        cost_estimate=cost(4 * rows * full, 18 * rows * full),
        name="blend",
    )(t, *terms, left_stat, right_stat, *done)


def around(x, k):
    n = lax.axis_size("tensor")
    return lax.ppermute(x, "tensor", [(i, (i + k) % n) for i in range(n)])


def exchange(x):
    return lax.all_to_all(x, "fsdp", split_axis=0, concat_axis=0, tiled=True)


def on_device(gradient, left_stat, right_stat, left_root, right_root, block_owner):
    owners = lax.axis_size("fsdp")
    t = lax.axis_index("tensor").reshape(1)
    routed, *cuts = route(t, block_owner, gradient, left_root, right_root, owners)
    cut_below, cut_far, cut_above = (around(c, k) for c, k in zip(cuts, (1, 2, 3)))
    owned = exchange(routed)
    owned, token = lax.optimization_barrier((owned, hold(cut_below, cut_above)))
    for_neighbours, for_opposite = select(t, owned)
    below, above = around(for_neighbours, 1), around(for_neighbours, -1)
    cuts = (cut_below, cut_above, cut_far)
    raw, square, left = own_part(t, token, left_root, right_root, cuts, owned)
    raw, for_opposite = lax.optimization_barrier((raw, for_opposite))
    far = around(for_opposite, 2)
    raw = near_part(raw, left, below, above, cut_below, cut_above)
    mine, after, before, sums = far_part(t, raw, square, left, far, cut_far)
    first, second = around(after, 1), around(before, -1)
    everyone = [sums] + [around(sums, k) for k in (1, 2, 3)]
    others = (below, above, far)
    terms = neighbour_terms(t, owned, others)
    everyone, terms = lax.optimization_barrier((everyone, terms))
    terms = around(terms[0], 1), around(terms[1], -1)
    returned = exchange(scale(t, mine, first, second, everyone, routed.shape))
    done = statistics(t, owned, others, left_stat, right_stat)
    new_left, new_right = blend(t, terms, left_stat, right_stat, done)
    return (new_left, new_right, collect(block_owner, returned))


def solution(mesh):
    return jax.shard_map(
        on_device,
        mesh=mesh,
        in_specs=(
            P(None, "fsdp", "tensor"),
            P("fsdp", "tensor", None),
            P("fsdp", "tensor", None),
            P("fsdp", "tensor", None),
            P("fsdp", "tensor", None),
            P(),
        ),
        out_specs=(P("fsdp", "tensor", None), P("fsdp", "tensor", None), P(None, "fsdp", "tensor")),
        check_vma=False,
    )
```

```python
import functools

import jax
import jax.numpy as jnp
from jax import lax
from jax.experimental import pallas as pl
from jax.experimental.pallas import tpu as pltpu
from jax.sharding import PartitionSpec as P

DECAY = 0.99
EPSILON = 1e-06
BF16 = jnp.bfloat16
F32 = jnp.float32
VMEM_SPEC = pl.BlockSpec(memory_space=pltpu.VMEM)
SMEM_SPEC = pl.BlockSpec(memory_space=pltpu.SMEM)
HBM_SPEC = pl.BlockSpec(memory_space=pltpu.HBM)
PARAMS = pltpu.CompilerParams(vmem_limit_bytes=20 * 1024 * 1024)
WHOLE = pltpu.CompilerParams(vmem_limit_bytes=63 * 1024 * 1024)


def dot(a, b, ca=1, cb=0):
    return lax.dot_general(a, b, (((ca,), (cb,)), ((), ())), preferred_element_type=F32)


def cost(flops, nbytes):
    return pl.CostEstimate(flops=flops, bytes_accessed=nbytes, transcendentals=0)


def clear_counts(count_ref, owners):
    def clear(i, _):
        count_ref[i] = 0
        return 0

    lax.fori_loop(0, owners, clear, 0, unroll=8)


def column_groups(member, width):
    half = width // 2
    after, before = lax.rem(member + 1, 4), lax.rem(member + 3, 4)
    return (member * width, width, 0), (after * width, half, width), (before * width + half, half, width + half)


def route_kernel(
    t_ref, owner_hbm, grad_hbm, left_hbm, right_hbm, out_hbm, c1, c2, c3,
    grad, out, left, right, owner_ref, count_ref, sems,
):
    bring = [
        pltpu.make_async_copy(owner_hbm, owner_ref, sems.at[0]),
        pltpu.make_async_copy(grad_hbm, grad, sems.at[1]),
        pltpu.make_async_copy(left_hbm, left, sems.at[2]),
        pltpu.make_async_copy(right_hbm, right, sems.at[3]),
    ]
    for c in bring:
        c.start()
    out[...] = jnp.zeros_like(out)
    clear_counts(count_ref, out.shape[0])
    for c in bring:
        c.wait()
    rows = left.shape[1]
    half = rows // 2
    width = right.shape[2] // 4
    sends = []
    for k, cut in ((1, c1), (2, c2), (3, c3)):
        d = lax.rem(t_ref[0] + k, 4)
        slot = lax.rem(d, 2)
        pieces = [(left.at[slot], cut.at[pl.ds(0, rows)])]
        for j in range(2):
            for start, size, at in column_groups(d, width):
                source = right.at[slot, pl.ds(j * half, half), pl.ds(pl.multiple_of(start, 128), size)]
                at = at + j * width if size == width else at + (j + 1) * width
                pieces.append((source, cut.at[pl.ds(rows, half), pl.ds(at, size)]))
        for i, (source, place) in enumerate(pieces):
            sends.append(pltpu.make_async_copy(source, place, sems.at[4 + 7 * (k - 1) + i]))
    for c in sends:
        c.start()

    def body(b, _):
        o = owner_ref[b]
        c = count_ref[o]
        count_ref[o] = c + 1
        out[o, c] = grad[b]
        return 0

    lax.fori_loop(0, grad.shape[0], body, 0, unroll=8)
    sends.append(pltpu.make_async_copy(out, out_hbm, sems.at[25]))
    sends[-1].start()
    for c in sends:
        c.wait()


def route(t, block_owner, gradient, left_root, right_root, owners):
    blocks, rows, cols = gradient.shape
    shape = (owners, 2, rows, cols)
    _, held, full = left_root.shape
    cut = jax.ShapeDtypeStruct((held + held // 2, full), BF16)
    return pl.pallas_call(
        route_kernel,
        out_shape=(jax.ShapeDtypeStruct(shape, gradient.dtype), cut, cut, cut),
        in_specs=[SMEM_SPEC] + [HBM_SPEC] * 4,
        out_specs=(HBM_SPEC,) * 4,
        scratch_shapes=[
            pltpu.VMEM(gradient.shape, BF16),
            pltpu.VMEM(shape, BF16),
            pltpu.VMEM(left_root.shape, BF16),
            pltpu.VMEM(right_root.shape, BF16),
            pltpu.SMEM((blocks,), jnp.int32),
            pltpu.SMEM((owners,), jnp.int32),
            pltpu.SemaphoreType.DMA((26,)),
        ],
        compiler_params=WHOLE,
        cost_estimate=cost(0, 3 * gradient.size),
        name="route",
    )(t, block_owner, gradient, left_root, right_root)


def collect_kernel(owner_hbm, slots_hbm, out_hbm, slots, out, owner_ref, count_ref, sems):
    bring = [
        pltpu.make_async_copy(owner_hbm, owner_ref, sems.at[0]),
        pltpu.make_async_copy(slots_hbm, slots, sems.at[1]),
    ]
    for c in bring:
        c.start()
    clear_counts(count_ref, slots.shape[0])
    for c in bring:
        c.wait()

    def body(b, _):
        o = owner_ref[b]
        c = count_ref[o]
        count_ref[o] = c + 1
        out[b] = slots[o, c]
        return 0

    lax.fori_loop(0, out.shape[0], body, 0, unroll=8)
    send = pltpu.make_async_copy(out, out_hbm, sems.at[2])
    send.start()
    send.wait()


def collect(block_owner, slots):
    blocks = block_owner.shape[0]
    shape = (blocks,) + slots.shape[2:]
    return pl.pallas_call(
        collect_kernel,
        out_shape=jax.ShapeDtypeStruct(shape, slots.dtype),
        in_specs=[HBM_SPEC] * 2,
        out_specs=HBM_SPEC,
        scratch_shapes=[
            pltpu.VMEM(slots.shape, slots.dtype),
            pltpu.VMEM(shape, slots.dtype),
            pltpu.SMEM((blocks,), jnp.int32),
            pltpu.SMEM((slots.shape[0],), jnp.int32),
            pltpu.SemaphoreType.DMA((3,)),
        ],
        compiler_params=PARAMS,
        cost_estimate=cost(0, 3 * slots.size),
        name="collect",
    )(block_owner, slots)


def select_kernel(t_ref, both_hbm, other_hbm, same_hbm, both, sems):
    bring = pltpu.make_async_copy(both_hbm, both, sems.at[0])
    bring.start()
    bring.wait()
    slot = lax.rem(t_ref[0], 2)
    sends = [
        pltpu.make_async_copy(both.at[:, 1 - slot], other_hbm, sems.at[1]),
        pltpu.make_async_copy(both.at[:, slot], same_hbm, sems.at[2]),
    ]
    for c in sends:
        c.start()
    for c in sends:
        c.wait()


def select(t, both):
    owners, _, height, width = both.shape
    out = jax.ShapeDtypeStruct((owners, height, width), BF16)
    return pl.pallas_call(
        select_kernel,
        out_shape=(out,) * 2,
        in_specs=[SMEM_SPEC, HBM_SPEC],
        out_specs=(HBM_SPEC,) * 2,
        scratch_shapes=[pltpu.VMEM(both.shape, BF16), pltpu.SemaphoreType.DMA((3,))],
        compiler_params=PARAMS,
        cost_estimate=cost(0, 4 * both.size),
        name="select",
    )(t, both)


def bring_right(cut, to, sems):
    _, rows, width = to.shape
    half = rows // 2
    return [
        pltpu.make_async_copy(
            cut.at[pl.ds(rows, half), pl.ds((2 * i + j) * width, width)],
            to.at[i, pl.ds(j * half, half)],
            sems.at[2 * i + j],
        )
        for i in range(2)
        for j in range(2)
    ]


def hold_kernel(a, b, out_ref):
    out_ref[...] = jnp.zeros_like(out_ref)


def hold(first, second):
    return pl.pallas_call(
        hold_kernel,
        out_shape=jax.ShapeDtypeStruct((8, 128), F32),
        in_specs=[HBM_SPEC] * 2,
        out_specs=VMEM_SPEC,
        compiler_params=WHOLE,
        cost_estimate=cost(2 * 10**11, 8 * 128),
        name="hold",
    )(first, second)


def own_kernel(
    t_ref, token, left_hbm, right_hbm, c1, c3, c2, both_hbm, raw_ref, square_ref, left, both, roots, sems
):
    t = t_ref[0]
    slot = lax.rem(t, 2)
    rows = left_hbm.shape[1]
    full = left.shape[0]
    width = roots.shape[2]
    bring = [
        pltpu.make_async_copy(both_hbm, both, sems.at[0]),
        pltpu.make_async_copy(left_hbm.at[slot], left.at[pl.ds(0, rows)], sems.at[1]),
    ]
    for i, c in enumerate((c1, c3, c2)):
        to = left.at[pl.ds((i + 1) * rows, rows)]
        bring.append(pltpu.make_async_copy(c.at[pl.ds(0, rows)], to, sems.at[2 + i]))
    for i, (start, size, at) in enumerate(column_groups(t, width)):
        source = right_hbm.at[slot, :, pl.ds(pl.multiple_of(start, 128), size)]
        to = roots.at[at // width, :, pl.ds(at % width, size)]
        bring.append(pltpu.make_async_copy(source, to, sems.at[5 + i]))
    for c in bring:
        c.start()
    for c in bring:
        c.wait()
    part = dot(left[...], both[:, slot].reshape(full, width)).astype(BF16)
    for i in range(2):
        raw_ref[i] = dot(part, roots[i])
    for i in range(2):
        wide = both[:, i].reshape(full, width).astype(F32)
        square_ref[i] = jnp.broadcast_to(jnp.sum(wide * wide, keepdims=True), square_ref.shape[1:])


def own_part(t, token, left_root, right_root, cuts, owned):
    owners, slots, height, width = owned.shape
    full = owners * height
    return pl.pallas_call(
        own_kernel,
        out_shape=(
            jax.ShapeDtypeStruct((2, full, width), F32),
            jax.ShapeDtypeStruct((slots, 8, 128), F32),
            jax.ShapeDtypeStruct((full, full), BF16),
        ),
        in_specs=[SMEM_SPEC, VMEM_SPEC] + [HBM_SPEC] * 6,
        out_specs=(VMEM_SPEC,) * 3,
        scratch_shapes=[
            pltpu.VMEM(owned.shape, BF16),
            pltpu.VMEM((2, width, width), BF16),
            pltpu.SemaphoreType.DMA((8,)),
        ],
        compiler_params=PARAMS,
        cost_estimate=cost(4 * full * full * width, 12 * full * full),
        name="own_part",
    )(t, token, left_root, right_root, *cuts, owned)


def rest_kernel(
    t_ref, own, square, left, g1, g3, g2, c1, c3, c2, mine_ref, after_ref, before_ref, sums_ref, roots, sems
):
    groups = [bring_right(c, roots.at[i], sems.at[i]) for i, c in enumerate((c1, c3, c2))]
    for bring in groups:
        for c in bring:
            c.start()
    full = left.shape[0]
    width = roots.shape[3]
    mine, other = own[0], own[1]
    for i, g in enumerate((g1, g3, g2)):
        part = dot(left[...], g[...].reshape(full, width)).astype(BF16)
        for c in groups[i]:
            c.wait()
        mine = mine + dot(part, roots[i, 0])
        other = other + dot(part, roots[i, 1])
    mine_ref[...] = mine
    after_ref[...] = other[:, : width // 2].astype(BF16)
    before_ref[...] = other[:, width // 2 :].astype(BF16)
    total = jnp.sum(mine * mine, keepdims=True) + jnp.sum(other * other, keepdims=True)
    row = lax.broadcasted_iota(jnp.int32, sums_ref.shape, 0)
    sums = jnp.where(row == lax.rem(t_ref[0], 2), total, jnp.zeros(sums_ref.shape, F32))
    for slot in range(2):
        sums = jnp.where(row == 2 + slot, square[slot], sums)
    sums_ref[...] = sums


def rest_part(t, own, square, left, grads, cuts):
    _, full, width = own.shape
    half = jax.ShapeDtypeStruct((full, width // 2), BF16)
    return pl.pallas_call(
        rest_kernel,
        out_shape=(
            jax.ShapeDtypeStruct((full, width), F32),
            half,
            half,
            jax.ShapeDtypeStruct((8, 128), F32),
        ),
        in_specs=[SMEM_SPEC] + [VMEM_SPEC] * 6 + [HBM_SPEC] * 3,
        out_specs=(VMEM_SPEC,) * 4,
        scratch_shapes=[pltpu.VMEM((3, 2, width, width), BF16), pltpu.SemaphoreType.DMA((3, 4))],
        compiler_params=PARAMS,
        cost_estimate=cost(9 * full * full * width, 12 * full * full),
        name="rest_part",
    )(t, own, square, left, *grads, *cuts)


def scale_kernel(t_ref, mine, first, second, s0, s1, s2, s3, out_hbm, ready, halves, sems):
    _, here, height, width = ready.shape
    rows = here * height
    t = t_ref[0]
    sums = s0[...] + s1[...] + s2[...] + s3[...]
    grafts = [
        jnp.sqrt((sums[2 + slot : 3 + slot, 0:1] + EPSILON) / (sums[slot : slot + 1, 0:1] + EPSILON))
        for slot in range(2)
    ]
    even = lax.rem(t, 2) == 0
    own_graft = jnp.where(even, grafts[0], grafts[1])
    other_graft = jnp.where(even, grafts[1], grafts[0])
    slot = lax.rem(t, 2)
    half = width // 2
    parts = (
        (mine, t, own_graft, slot, ready, pl.ds(0, width)),
        (first, t + 3, other_graft, 1 - slot, halves.at[0], pl.ds(0, half)),
        (second, t + 1, other_graft, 1 - slot, halves.at[1], pl.ds(half, half)),
    )
    copies = []
    for j, (raw, member, graft, slot, held, cols) in enumerate(parts):
        for i, k in enumerate((0, 1, 3, 2)):
            scaled = raw[i * rows : (i + 1) * rows, :].astype(F32) * graft
            held[i] = scaled.astype(BF16).reshape(here, height, held.shape[3])
            s = lax.rem(member + 4 - k, 4)
            to = out_hbm.at[pl.ds(s * here, here), slot, :, cols]
            copies.append(pltpu.make_async_copy(held.at[i], to, sems.at[j, i]))
            copies[-1].start()
    for c in copies:
        c.wait()


def scale(t, mine, first, second, sums, shape):
    owners, _, height, width = shape
    here = owners // 4
    return pl.pallas_call(
        scale_kernel,
        out_shape=jax.ShapeDtypeStruct(shape, BF16),
        in_specs=[SMEM_SPEC] + [VMEM_SPEC] * 7,
        out_specs=HBM_SPEC,
        scratch_shapes=[
            pltpu.VMEM((4, here, height, width), BF16),
            pltpu.VMEM((2, 4, here, height, width // 2), BF16),
            pltpu.SemaphoreType.DMA((3, 4)),
        ],
        compiler_params=PARAMS,
        cost_estimate=cost(0, 16 * owners * height * width),
        name="scale",
    )(t, mine, first, second, *sums)


def terms_kernel(t_ref, g0_hbm, g1, g3, g2, left_ref, right_ref, own, sems):
    t = t_ref[0]
    bring = pltpu.make_async_copy(g0_hbm.at[:, lax.rem(t, 2)], own, sems.at[0])
    bring.start()
    owners, height, rows = own.shape
    full = owners * height
    here = owners // 4
    after = pl.ds(pl.multiple_of(lax.rem(t + 1, 4) * here, here), here)
    turned = g1[...].reshape(full, rows).T
    bring.wait()
    term = None
    for k, g in ((0, own), (1, g1), (3, g3), (2, g2)):
        whole = g[...].reshape(full, rows)
        part = dot(g[after].reshape(rows, rows), whole, 1, 1)
        term = part if term is None else term + part
        s = lax.rem(t + 4 - k, 4)
        cols = pl.ds(pl.multiple_of(s * rows, rows), rows)
        right_ref[:, cols] = dot(turned, whole).astype(BF16)
    left_ref[...] = term.astype(BF16)


def neighbour_terms(t, owned, others):
    owners, _, height, rows = owned.shape
    out = jax.ShapeDtypeStruct((rows, owners * height), BF16)
    return pl.pallas_call(
        terms_kernel,
        out_shape=(out, out),
        in_specs=[SMEM_SPEC, HBM_SPEC] + [VMEM_SPEC] * 3,
        out_specs=(VMEM_SPEC, VMEM_SPEC),
        scratch_shapes=[pltpu.VMEM((owners, height, rows), BF16), pltpu.SemaphoreType.DMA((1,))],
        compiler_params=PARAMS,
        cost_estimate=cost(4 * rows * (owners * height) ** 2, 6 * rows * owners * height),
        name="neighbour_terms",
    )(t, owned, *others)


def stats_kernel(t_ref, g0_hbm, g1, g3, g2, left_ref, right_ref, new_left_ref, new_right_ref, own, sems):
    t = t_ref[0]
    rows, full = left_ref.shape
    here = own.shape[0] // 4
    mine = pl.ds(pl.multiple_of(t * here, here), here)
    bring = pltpu.make_async_copy(g0_hbm.at[:, lax.rem(t, 2)], own, sems.at[0])
    bring.start()
    bring.wait()
    turned = own[...].reshape(full, rows).T
    term = None
    for k, g in ((0, own), (1, g1), (3, g3), (2, g2)):
        whole = g[...].reshape(full, rows)
        part = dot(g[mine].reshape(rows, rows), whole, 1, 1)
        term = part if term is None else term + part
        s = lax.rem(t + 4 - k, 4)
        cols = pl.ds(pl.multiple_of(s * rows, rows), rows)
        new_right_ref[:, cols] = DECAY * right_ref[:, cols] + (1.0 - DECAY) * dot(turned, whole)
    new_left_ref[...] = DECAY * left_ref[...] + (1.0 - DECAY) * term


def statistics(t, owned, others, left_stat, right_stat):
    _, rows, full = left_stat.shape
    owners, _, height, width = owned.shape
    slot_spec = pl.BlockSpec((None, rows, full), lambda i, t_ref: (lax.rem(t_ref[0], 2), 0, 0))
    shape = jax.ShapeDtypeStruct(left_stat.shape, F32)
    return pl.pallas_call(
        stats_kernel,
        out_shape=(shape, shape),
        grid_spec=pltpu.PrefetchScalarGridSpec(
            num_scalar_prefetch=1,
            grid=(1,),
            in_specs=[HBM_SPEC] + [VMEM_SPEC] * 3 + [slot_spec] * 2,
            out_specs=(slot_spec, slot_spec),
            scratch_shapes=[pltpu.VMEM((owners, height, width), BF16), pltpu.SemaphoreType.DMA((1,))],
        ),
        compiler_params=pltpu.CompilerParams(vmem_limit_bytes=32 * 1024 * 1024),
        cost_estimate=cost(4 * rows * full * full, 12 * rows * full),
        name="statistics",
    )(t, owned, *others, left_stat, right_stat)


def blend_kernel(t_ref, left_term, right_term, left_ref, right_ref, _, __, new_left_ref, new_right_ref):
    new_left_ref[...] = DECAY * left_ref[...] + (1.0 - DECAY) * left_term[...].astype(F32)
    new_right_ref[...] = DECAY * right_ref[...] + (1.0 - DECAY) * right_term[...].astype(F32)


def blend(t, terms, left_stat, right_stat, done):
    _, rows, full = left_stat.shape
    slot_spec = pl.BlockSpec((None, rows, full), lambda i, t_ref: (1 - lax.rem(t_ref[0], 2), 0, 0))
    shape = jax.ShapeDtypeStruct(left_stat.shape, F32)
    return pl.pallas_call(
        blend_kernel,
        out_shape=(shape, shape),
        grid_spec=pltpu.PrefetchScalarGridSpec(
            num_scalar_prefetch=1,
            grid=(1,),
            in_specs=[VMEM_SPEC] * 2 + [slot_spec] * 2 + [HBM_SPEC] * 2,
            out_specs=(slot_spec, slot_spec),
        ),
        input_output_aliases={5: 0, 6: 1},
        compiler_params=pltpu.CompilerParams(vmem_limit_bytes=32 * 1024 * 1024),
        cost_estimate=cost(4 * rows * full, 18 * rows * full),
        name="blend",
    )(t, *terms, left_stat, right_stat, *done)


def around(x, k):
    n = lax.axis_size("tensor")
    return lax.ppermute(x, "tensor", [(i, (i + k) % n) for i in range(n)])


def exchange(x):
    return lax.all_to_all(x, "fsdp", split_axis=0, concat_axis=0, tiled=True)


def on_device(gradient, left_stat, right_stat, left_root, right_root, block_owner):
    owners = lax.axis_size("fsdp")
    t = lax.axis_index("tensor").reshape(1)
    routed, *cuts = route(t, block_owner, gradient, left_root, right_root, owners)
    cut_below, cut_far, cut_above = (around(c, k) for c, k in zip(cuts, (1, 2, 3)))
    owned = exchange(routed)
    owned, token = lax.optimization_barrier((owned, hold(cut_below, cut_above)))
    for_neighbours, for_opposite = select(t, owned)
    below, above = around(for_neighbours, 1), around(for_neighbours, -1)
    cuts = (cut_below, cut_above, cut_far)
    raw, square, left = own_part(t, token, left_root, right_root, cuts, owned)
    far = around(for_opposite, 2)
    mine, after, before, sums = rest_part(t, raw, square, left, (below, above, far), cuts)
    first, second = around(after, 1), around(before, -1)
    everyone = [sums] + [around(sums, k) for k in (1, 2, 3)]
    others = (below, above, far)
    scaled = scale(t, mine, first, second, everyone, routed.shape)
    scaled, late = lax.optimization_barrier((scaled, owned))
    returned = exchange(scaled)
    terms = neighbour_terms(t, late, others)
    terms = around(terms[0], 1), around(terms[1], -1)
    done = statistics(t, owned, others, left_stat, right_stat)
    new_left, new_right = blend(t, terms, left_stat, right_stat, done)
    return (new_left, new_right, collect(block_owner, returned))


def solution(mesh):
    return jax.shard_map(
        on_device,
        mesh=mesh,
        in_specs=(
            P(None, "fsdp", "tensor"),
            P("fsdp", "tensor", None),
            P("fsdp", "tensor", None),
            P("fsdp", "tensor", None),
            P("fsdp", "tensor", None),
            P(),
        ),
        out_specs=(P("fsdp", "tensor", None), P("fsdp", "tensor", None), P(None, "fsdp", "tensor")),
        check_vma=False,
    )
```

```python
import functools

import jax
import jax.numpy as jnp
from jax import lax
from jax.experimental import pallas as pl
from jax.experimental.pallas import tpu as pltpu
from jax.sharding import PartitionSpec as P

DECAY = 0.99
EPSILON = 1e-06
BF16 = jnp.bfloat16
F32 = jnp.float32
VMEM_SPEC = pl.BlockSpec(memory_space=pltpu.VMEM)
SMEM_SPEC = pl.BlockSpec(memory_space=pltpu.SMEM)
HBM_SPEC = pl.BlockSpec(memory_space=pltpu.HBM)
PARAMS = pltpu.CompilerParams(vmem_limit_bytes=20 * 1024 * 1024)
WHOLE = pltpu.CompilerParams(vmem_limit_bytes=63 * 1024 * 1024)


def dot(a, b, ca=1, cb=0):
    return lax.dot_general(a, b, (((ca,), (cb,)), ((), ())), preferred_element_type=F32)


def cost(flops, nbytes):
    return pl.CostEstimate(flops=flops, bytes_accessed=nbytes, transcendentals=0)


def clear_counts(count_ref, owners):
    def clear(i, _):
        count_ref[i] = 0
        return 0

    lax.fori_loop(0, owners, clear, 0, unroll=8)


def column_groups(member, width):
    half = width // 2
    after, before = lax.rem(member + 1, 4), lax.rem(member + 3, 4)
    return (member * width, width, 0), (after * width, half, width), (before * width + half, half, width + half)


def route_kernel(
    t_ref, owner_hbm, grad_hbm, left_hbm, right_hbm, out_hbm, c1, c2, c3,
    grad, out, left, right, owner_ref, count_ref, sems,
):
    bring = [
        pltpu.make_async_copy(owner_hbm, owner_ref, sems.at[0]),
        pltpu.make_async_copy(grad_hbm, grad, sems.at[1]),
        pltpu.make_async_copy(left_hbm, left, sems.at[2]),
        pltpu.make_async_copy(right_hbm, right, sems.at[3]),
    ]
    for c in bring:
        c.start()
    out[...] = jnp.zeros_like(out)
    clear_counts(count_ref, out.shape[0])
    for c in bring:
        c.wait()
    rows = left.shape[1]
    half = rows // 2
    width = right.shape[2] // 4
    sends = []
    for k, cut in ((1, c1), (2, c2), (3, c3)):
        d = lax.rem(t_ref[0] + k, 4)
        slot = lax.rem(d, 2)
        pieces = [(left.at[slot], cut.at[pl.ds(0, rows)])]
        for j in range(2):
            for start, size, at in column_groups(d, width):
                source = right.at[slot, pl.ds(j * half, half), pl.ds(pl.multiple_of(start, 128), size)]
                at = at + j * width if size == width else at + (j + 1) * width
                pieces.append((source, cut.at[pl.ds(rows, half), pl.ds(at, size)]))
        for i, (source, place) in enumerate(pieces):
            sends.append(pltpu.make_async_copy(source, place, sems.at[4 + 7 * (k - 1) + i]))
    for c in sends:
        c.start()

    def body(b, _):
        o = owner_ref[b]
        c = count_ref[o]
        count_ref[o] = c + 1
        out[o, c] = grad[b]
        return 0

    lax.fori_loop(0, grad.shape[0], body, 0, unroll=8)
    sends.append(pltpu.make_async_copy(out, out_hbm, sems.at[25]))
    sends[-1].start()
    for c in sends:
        c.wait()


def route(t, block_owner, gradient, left_root, right_root, owners):
    blocks, rows, cols = gradient.shape
    shape = (owners, 2, rows, cols)
    _, held, full = left_root.shape
    cut = jax.ShapeDtypeStruct((held + held // 2, full), BF16)
    return pl.pallas_call(
        route_kernel,
        out_shape=(jax.ShapeDtypeStruct(shape, gradient.dtype), cut, cut, cut),
        in_specs=[SMEM_SPEC] + [HBM_SPEC] * 4,
        out_specs=(HBM_SPEC,) * 4,
        scratch_shapes=[
            pltpu.VMEM(gradient.shape, BF16),
            pltpu.VMEM(shape, BF16),
            pltpu.VMEM(left_root.shape, BF16),
            pltpu.VMEM(right_root.shape, BF16),
            pltpu.SMEM((blocks,), jnp.int32),
            pltpu.SMEM((owners,), jnp.int32),
            pltpu.SemaphoreType.DMA((26,)),
        ],
        compiler_params=WHOLE,
        cost_estimate=cost(0, 3 * gradient.size),
        name="route",
    )(t, block_owner, gradient, left_root, right_root)


def collect_kernel(owner_hbm, slots_hbm, out_hbm, slots, out, owner_ref, count_ref, sems):
    bring = [
        pltpu.make_async_copy(owner_hbm, owner_ref, sems.at[0]),
        pltpu.make_async_copy(slots_hbm, slots, sems.at[1]),
    ]
    for c in bring:
        c.start()
    clear_counts(count_ref, slots.shape[0])
    for c in bring:
        c.wait()

    def body(b, _):
        o = owner_ref[b]
        c = count_ref[o]
        count_ref[o] = c + 1
        out[b] = slots[o, c]
        return 0

    lax.fori_loop(0, out.shape[0], body, 0, unroll=8)
    send = pltpu.make_async_copy(out, out_hbm, sems.at[2])
    send.start()
    send.wait()


def collect(block_owner, slots):
    blocks = block_owner.shape[0]
    shape = (blocks,) + slots.shape[2:]
    return pl.pallas_call(
        collect_kernel,
        out_shape=jax.ShapeDtypeStruct(shape, slots.dtype),
        in_specs=[HBM_SPEC] * 2,
        out_specs=HBM_SPEC,
        scratch_shapes=[
            pltpu.VMEM(slots.shape, slots.dtype),
            pltpu.VMEM(shape, slots.dtype),
            pltpu.SMEM((blocks,), jnp.int32),
            pltpu.SMEM((slots.shape[0],), jnp.int32),
            pltpu.SemaphoreType.DMA((3,)),
        ],
        compiler_params=PARAMS,
        cost_estimate=cost(0, 3 * slots.size),
        name="collect",
    )(block_owner, slots)


def select_kernel(t_ref, both_hbm, other_hbm, same_hbm, both, sems):
    bring = pltpu.make_async_copy(both_hbm, both, sems.at[0])
    bring.start()
    bring.wait()
    slot = lax.rem(t_ref[0], 2)
    sends = [
        pltpu.make_async_copy(both.at[:, 1 - slot], other_hbm, sems.at[1]),
        pltpu.make_async_copy(both.at[:, slot], same_hbm, sems.at[2]),
    ]
    for c in sends:
        c.start()
    for c in sends:
        c.wait()


def select(t, both):
    owners, _, height, width = both.shape
    out = jax.ShapeDtypeStruct((owners, height, width), BF16)
    return pl.pallas_call(
        select_kernel,
        out_shape=(out,) * 2,
        in_specs=[SMEM_SPEC, HBM_SPEC],
        out_specs=(HBM_SPEC,) * 2,
        scratch_shapes=[pltpu.VMEM(both.shape, BF16), pltpu.SemaphoreType.DMA((3,))],
        compiler_params=PARAMS,
        cost_estimate=cost(0, 4 * both.size),
        name="select",
    )(t, both)


def bring_right(cut, to, sems):
    _, rows, width = to.shape
    half = rows // 2
    return [
        pltpu.make_async_copy(
            cut.at[pl.ds(rows, half), pl.ds((2 * i + j) * width, width)],
            to.at[i, pl.ds(j * half, half)],
            sems.at[2 * i + j],
        )
        for i in range(2)
        for j in range(2)
    ]


def hold_kernel(a, b, out_ref):
    out_ref[...] = jnp.zeros_like(out_ref)


def hold(first, second):
    return pl.pallas_call(
        hold_kernel,
        out_shape=jax.ShapeDtypeStruct((8, 128), F32),
        in_specs=[HBM_SPEC] * 2,
        out_specs=VMEM_SPEC,
        compiler_params=WHOLE,
        cost_estimate=cost(2 * 10**11, 8 * 128),
        name="hold",
    )(first, second)


def own_kernel(
    t_ref, token, left_hbm, right_hbm, c1, c3, c2, both_hbm, raw_ref, square_ref, left, both, roots, sems
):
    t = t_ref[0]
    slot = lax.rem(t, 2)
    rows = left_hbm.shape[1]
    full = left.shape[0]
    width = roots.shape[2]
    bring = [
        pltpu.make_async_copy(both_hbm, both, sems.at[0]),
        pltpu.make_async_copy(left_hbm.at[slot], left.at[pl.ds(0, rows)], sems.at[1]),
    ]
    for i, c in enumerate((c1, c3, c2)):
        to = left.at[pl.ds((i + 1) * rows, rows)]
        bring.append(pltpu.make_async_copy(c.at[pl.ds(0, rows)], to, sems.at[2 + i]))
    for i, (start, size, at) in enumerate(column_groups(t, width)):
        source = right_hbm.at[slot, :, pl.ds(pl.multiple_of(start, 128), size)]
        to = roots.at[at // width, :, pl.ds(at % width, size)]
        bring.append(pltpu.make_async_copy(source, to, sems.at[5 + i]))
    for c in bring:
        c.start()
    for c in bring:
        c.wait()
    part = dot(left[...], both[:, slot].reshape(full, width)).astype(BF16)
    for i in range(2):
        raw_ref[i] = dot(part, roots[i])
    for i in range(2):
        wide = both[:, i].reshape(full, width).astype(F32)
        square_ref[i] = jnp.broadcast_to(jnp.sum(wide * wide, keepdims=True), square_ref.shape[1:])


def own_part(t, token, left_root, right_root, cuts, owned):
    owners, slots, height, width = owned.shape
    full = owners * height
    return pl.pallas_call(
        own_kernel,
        out_shape=(
            jax.ShapeDtypeStruct((2, full, width), F32),
            jax.ShapeDtypeStruct((slots, 8, 128), F32),
            jax.ShapeDtypeStruct((full, full), BF16),
        ),
        in_specs=[SMEM_SPEC, VMEM_SPEC] + [HBM_SPEC] * 6,
        out_specs=(VMEM_SPEC,) * 3,
        scratch_shapes=[
            pltpu.VMEM(owned.shape, BF16),
            pltpu.VMEM((2, width, width), BF16),
            pltpu.SemaphoreType.DMA((8,)),
        ],
        compiler_params=PARAMS,
        cost_estimate=cost(4 * full * full * width, 12 * full * full),
        name="own_part",
    )(t, token, left_root, right_root, *cuts, owned)


def three_parts(value):
    high = value.astype(BF16)
    rest = value - high.astype(F32)
    middle = rest.astype(BF16)
    return high, middle, (rest - middle.astype(F32)).astype(BF16)


def rest_kernel(
    t_ref, own, square, left, g1, g3, g2, c1, c3, c2, mine_ref, after_ref, before_ref, sums_ref, roots, sems
):
    groups = [bring_right(c, roots.at[i], sems.at[i]) for i, c in enumerate((c1, c3, c2))]
    for bring in groups:
        for c in bring:
            c.start()
    full = left.shape[0]
    width = roots.shape[3]
    mine, other = own[0], own[1]
    for i, g in enumerate((g1, g3, g2)):
        part = dot(left[...], g[...].reshape(full, width)).astype(BF16)
        for c in groups[i]:
            c.wait()
        mine = mine + dot(part, roots[i, 0])
        other = other + dot(part, roots[i, 1])
    mine_ref[...] = mine
    after_ref[0:full, :] = other[:, : width // 2].astype(BF16)
    before_ref[0:full, :] = other[:, width // 2 :].astype(BF16)
    total = jnp.sum(mine * mine, keepdims=True) + jnp.sum(other * other, keepdims=True)
    row = lax.broadcasted_iota(jnp.int32, sums_ref.shape, 0)
    sums = jnp.where(row == lax.rem(t_ref[0], 2), total, jnp.zeros(sums_ref.shape, F32))
    for slot in range(2):
        sums = jnp.where(row == 2 + slot, square[slot], sums)
    sums_ref[...] = sums
    shape = (16, width // 2)
    row = lax.broadcasted_iota(jnp.int32, shape, 0)
    tile = jnp.zeros(shape, F32)
    for i, value in enumerate((total, square[0, 0:1, 0:1], square[1, 0:1, 0:1])):
        for j, part in enumerate(three_parts(jnp.broadcast_to(value, shape))):
            tile = jnp.where(row == 3 * i + j, part.astype(F32), tile)
    after_ref[full : full + 16, :] = tile.astype(BF16)
    before_ref[full : full + 16, :] = tile.astype(BF16)


def rest_part(t, own, square, left, grads, cuts):
    _, full, width = own.shape
    half = jax.ShapeDtypeStruct((full + 16, width // 2), BF16)
    return pl.pallas_call(
        rest_kernel,
        out_shape=(
            jax.ShapeDtypeStruct((full, width), F32),
            half,
            half,
            jax.ShapeDtypeStruct((8, 128), F32),
        ),
        in_specs=[SMEM_SPEC] + [VMEM_SPEC] * 6 + [HBM_SPEC] * 3,
        out_specs=(VMEM_SPEC,) * 4,
        scratch_shapes=[pltpu.VMEM((3, 2, width, width), BF16), pltpu.SemaphoreType.DMA((3, 4))],
        compiler_params=PARAMS,
        cost_estimate=cost(9 * full * full * width, 12 * full * full),
        name="rest_part",
    )(t, own, square, left, *grads, *cuts)


def scale_kernel(t_ref, mine, first, second, s0, s2, out_hbm, ready, halves, sems):
    _, here, height, width = ready.shape
    rows = here * height
    t = t_ref[0]
    sums = s0[...] + s2[...]
    tiles = [x[4 * rows : 4 * rows + 16, 0:1].astype(F32) for x in (first, second)]

    def sent(i):
        parts = [x[i : i + 1] + x[i + 1 : i + 2] + x[i + 2 : i + 3] for x in tiles]
        return parts[0] + parts[1]

    squares = [sums[2 + slot : 3 + slot, 0:1] + sent(3 + 3 * slot) for slot in range(2)]
    even = lax.rem(t, 2) == 0
    own_square = jnp.where(even, squares[0], squares[1])
    other_square = jnp.where(even, squares[1], squares[0])
    own_graft = jnp.sqrt((own_square + EPSILON) / (sums[0:1, 0:1] + sums[1:2, 0:1] + EPSILON))
    other_graft = jnp.sqrt((other_square + EPSILON) / (sent(0) + EPSILON))
    slot = lax.rem(t, 2)
    half = width // 2
    parts = (
        (mine, t, own_graft, slot, ready, pl.ds(0, width)),
        (first, t + 3, other_graft, 1 - slot, halves.at[0], pl.ds(0, half)),
        (second, t + 1, other_graft, 1 - slot, halves.at[1], pl.ds(half, half)),
    )
    copies = []
    for j, (raw, member, graft, slot, held, cols) in enumerate(parts):
        for i, k in enumerate((0, 1, 3, 2)):
            scaled = raw[i * rows : (i + 1) * rows, :].astype(F32) * graft
            held[i] = scaled.astype(BF16).reshape(here, height, held.shape[3])
            s = lax.rem(member + 4 - k, 4)
            to = out_hbm.at[pl.ds(s * here, here), slot, :, cols]
            copies.append(pltpu.make_async_copy(held.at[i], to, sems.at[j, i]))
            copies[-1].start()
    for c in copies:
        c.wait()


def scale(t, mine, first, second, sums, shape):
    owners, _, height, width = shape
    here = owners // 4
    return pl.pallas_call(
        scale_kernel,
        out_shape=jax.ShapeDtypeStruct(shape, BF16),
        in_specs=[SMEM_SPEC] + [VMEM_SPEC] * 5,
        out_specs=HBM_SPEC,
        scratch_shapes=[
            pltpu.VMEM((4, here, height, width), BF16),
            pltpu.VMEM((2, 4, here, height, width // 2), BF16),
            pltpu.SemaphoreType.DMA((3, 4)),
        ],
        compiler_params=PARAMS,
        cost_estimate=cost(0, 16 * owners * height * width),
        name="scale",
    )(t, mine, first, second, *sums)


def terms_kernel(t_ref, g0_hbm, g1, g3, g2, left_ref, right_ref, own, sems):
    t = t_ref[0]
    bring = pltpu.make_async_copy(g0_hbm.at[:, lax.rem(t, 2)], own, sems.at[0])
    bring.start()
    owners, height, rows = own.shape
    full = owners * height
    here = owners // 4
    after = pl.ds(pl.multiple_of(lax.rem(t + 1, 4) * here, here), here)
    turned = g1[...].reshape(full, rows).T
    bring.wait()
    term = None
    for k, g in ((0, own), (1, g1), (3, g3), (2, g2)):
        whole = g[...].reshape(full, rows)
        part = dot(g[after].reshape(rows, rows), whole, 1, 1)
        term = part if term is None else term + part
        s = lax.rem(t + 4 - k, 4)
        cols = pl.ds(pl.multiple_of(s * rows, rows), rows)
        right_ref[:, cols] = dot(turned, whole).astype(BF16)
    left_ref[...] = term.astype(BF16)


def neighbour_terms(t, owned, others):
    owners, _, height, rows = owned.shape
    out = jax.ShapeDtypeStruct((rows, owners * height), BF16)
    return pl.pallas_call(
        terms_kernel,
        out_shape=(out, out),
        in_specs=[SMEM_SPEC, HBM_SPEC] + [VMEM_SPEC] * 3,
        out_specs=(VMEM_SPEC, VMEM_SPEC),
        scratch_shapes=[pltpu.VMEM((owners, height, rows), BF16), pltpu.SemaphoreType.DMA((1,))],
        compiler_params=PARAMS,
        cost_estimate=cost(4 * rows * (owners * height) ** 2, 6 * rows * owners * height),
        name="neighbour_terms",
    )(t, owned, *others)


def stats_kernel(t_ref, g0_hbm, g1, g3, g2, left_ref, right_ref, new_left_ref, new_right_ref, own, sems):
    t = t_ref[0]
    rows, full = left_ref.shape
    here = own.shape[0] // 4
    mine = pl.ds(pl.multiple_of(t * here, here), here)
    bring = pltpu.make_async_copy(g0_hbm.at[:, lax.rem(t, 2)], own, sems.at[0])
    bring.start()
    bring.wait()
    turned = own[...].reshape(full, rows).T
    term = None
    for k, g in ((0, own), (1, g1), (3, g3), (2, g2)):
        whole = g[...].reshape(full, rows)
        part = dot(g[mine].reshape(rows, rows), whole, 1, 1)
        term = part if term is None else term + part
        s = lax.rem(t + 4 - k, 4)
        cols = pl.ds(pl.multiple_of(s * rows, rows), rows)
        new_right_ref[:, cols] = DECAY * right_ref[:, cols] + (1.0 - DECAY) * dot(turned, whole)
    new_left_ref[...] = DECAY * left_ref[...] + (1.0 - DECAY) * term


def statistics(t, owned, others, left_stat, right_stat):
    _, rows, full = left_stat.shape
    owners, _, height, width = owned.shape
    slot_spec = pl.BlockSpec((None, rows, full), lambda i, t_ref: (lax.rem(t_ref[0], 2), 0, 0))
    shape = jax.ShapeDtypeStruct(left_stat.shape, F32)
    return pl.pallas_call(
        stats_kernel,
        out_shape=(shape, shape),
        grid_spec=pltpu.PrefetchScalarGridSpec(
            num_scalar_prefetch=1,
            grid=(1,),
            in_specs=[HBM_SPEC] + [VMEM_SPEC] * 3 + [slot_spec] * 2,
            out_specs=(slot_spec, slot_spec),
            scratch_shapes=[pltpu.VMEM((owners, height, width), BF16), pltpu.SemaphoreType.DMA((1,))],
        ),
        compiler_params=pltpu.CompilerParams(vmem_limit_bytes=32 * 1024 * 1024),
        cost_estimate=cost(4 * rows * full * full, 12 * rows * full),
        name="statistics",
    )(t, owned, *others, left_stat, right_stat)


def blend_kernel(t_ref, left_term, right_term, left_ref, right_ref, _, __, new_left_ref, new_right_ref):
    new_left_ref[...] = DECAY * left_ref[...] + (1.0 - DECAY) * left_term[...].astype(F32)
    new_right_ref[...] = DECAY * right_ref[...] + (1.0 - DECAY) * right_term[...].astype(F32)


def blend(t, terms, left_stat, right_stat, done):
    _, rows, full = left_stat.shape
    slot_spec = pl.BlockSpec((None, rows, full), lambda i, t_ref: (1 - lax.rem(t_ref[0], 2), 0, 0))
    shape = jax.ShapeDtypeStruct(left_stat.shape, F32)
    return pl.pallas_call(
        blend_kernel,
        out_shape=(shape, shape),
        grid_spec=pltpu.PrefetchScalarGridSpec(
            num_scalar_prefetch=1,
            grid=(1,),
            in_specs=[VMEM_SPEC] * 2 + [slot_spec] * 2 + [HBM_SPEC] * 2,
            out_specs=(slot_spec, slot_spec),
        ),
        input_output_aliases={5: 0, 6: 1},
        compiler_params=pltpu.CompilerParams(vmem_limit_bytes=32 * 1024 * 1024),
        cost_estimate=cost(4 * rows * full, 18 * rows * full),
        name="blend",
    )(t, *terms, left_stat, right_stat, *done)


def around(x, k):
    n = lax.axis_size("tensor")
    return lax.ppermute(x, "tensor", [(i, (i + k) % n) for i in range(n)])


def exchange(x):
    return lax.all_to_all(x, "fsdp", split_axis=0, concat_axis=0, tiled=True)


def on_device(gradient, left_stat, right_stat, left_root, right_root, block_owner):
    owners = lax.axis_size("fsdp")
    t = lax.axis_index("tensor").reshape(1)
    routed, *cuts = route(t, block_owner, gradient, left_root, right_root, owners)
    cut_below, cut_far, cut_above = (around(c, k) for c, k in zip(cuts, (1, 2, 3)))
    owned = exchange(routed)
    owned, token = lax.optimization_barrier((owned, hold(cut_below, cut_above)))
    for_neighbours, for_opposite = select(t, owned)
    below, above = around(for_neighbours, 1), around(for_neighbours, -1)
    cuts = (cut_below, cut_above, cut_far)
    raw, square, left = own_part(t, token, left_root, right_root, cuts, owned)
    far = around(for_opposite, 2)
    mine, after, before, sums = rest_part(t, raw, square, left, (below, above, far), cuts)
    first, second = around(after, 1), around(before, -1)
    norms = sums, around(sums, 2)
    others = (below, above, far)
    scaled = scale(t, mine, first, second, norms, routed.shape)
    scaled, late = lax.optimization_barrier((scaled, owned))
    returned = exchange(scaled)
    terms = neighbour_terms(t, late, others)
    terms = around(terms[0], 1), around(terms[1], -1)
    done = statistics(t, owned, others, left_stat, right_stat)
    new_left, new_right = blend(t, terms, left_stat, right_stat, done)
    return (new_left, new_right, collect(block_owner, returned))


def solution(mesh):
    return jax.shard_map(
        on_device,
        mesh=mesh,
        in_specs=(
            P(None, "fsdp", "tensor"),
            P("fsdp", "tensor", None),
            P("fsdp", "tensor", None),
            P("fsdp", "tensor", None),
            P("fsdp", "tensor", None),
            P(),
        ),
        out_specs=(P("fsdp", "tensor", None), P("fsdp", "tensor", None), P(None, "fsdp", "tensor")),
        check_vma=False,
    )
```
